256 devices in a mesh: row: 4 (over y), col: 16 (over z, core), layer: 4 (over x).
Axes of the slice: x: 4, y: 4, z: 8, core: 2. Of those that a mesh axis runs over, the one named last changes fastest.
Arguments:
- density: bfloat16 [8192, 4, 2048], P('row', 'layer', 'col'), may hold values from -6 to 6
- response: bfloat16 [4, 2048, 8192], P('layer', 'row', 'col'), may hold values from -0.125 to 0.125
- density_mask: int32 [64, 4, 16], P('row', 'layer', 'col'), may hold values 0 or 1
- response_mask: int32 [4, 16, 64], P('layer', 'row', 'col'), may hold values 0 or 1
- result_mask: int32 [64, 64], P('row', 'col'), may hold values 0 or 1
Outputs:
- perturbed: bfloat16 [16, 16, 32, 8192], P(('row', 'layer'), 'col')
The draws below stay inside these ranges and needn't reach their ends.
All inputs are finite; a program needn't handle non-finite values. No bound on the sum of `density_mask` or of `response_mask` or of `result_mask` on one device may be relied on, other than what follows from the above.
Results may differ from the reference program's by a relative error of at most 0.0042.
Values may be sent and summed in bfloat16 or wider, within the bound.
No kernel may reach another device: no remote copies, remote signals or barrier semaphores. Data moves between devices by JAX's collectives and lax.ppermute only.
A program may use at most 64 MiB of HBM per device.

```python
import jax
import jax.numpy as jnp

ORDER = 8192
NBLK = 64
BANDS = 16
SLAB = 32
N_COL = 16
N_LAYER = 4


def with_ends(entries, key, low, high):
    longest = entries.shape.index(max(entries.shape))
    spots = []
    for shift in (0, 1):
        where = [jax.random.randint(jax.random.fold_in(key, axis), (), 0, length) for axis, length in enumerate(entries.shape)]
        where[longest] = (where[longest] + shift) % entries.shape[longest]
        spots.append(tuple(where))
    return entries.at[spots[0]].set(low).at[spots[1]].set(high)


def shard_levels(own_key, extent, split, least, top_value):
    def one(dim, blocks):
        heights = jax.random.uniform(jax.random.fold_in(jax.random.fold_in(own_key, 6), dim), (blocks,), jnp.float32, least / len(split), top_value / len(split))
        return jnp.repeat(jnp.exp(heights), extent[dim] // blocks).reshape((-1,) + (1,) * (len(extent) - dim - 1))

    level = one(*split[0])
    for cut in split[1:]:
        level = level * one(*cut)
    return level


def scatter_about(own_key, shape, spread, reach, cuts=(), held_as=jnp.bfloat16):
    result = spread * jax.random.normal(own_key, shape, jnp.float32)
    if cuts:
        result = result * shard_levels(own_key, shape, cuts, -0.22, 0.18)
    return jnp.clip(result, -reach, reach).astype(held_as)


def setup_inputs(seed: int = 0) -> dict:
    streams_of = jax.random.split(jax.random.key(seed), 6)
    density = scatter_about(streams_of[0], (ORDER, N_LAYER, ORDER // N_LAYER), 1.0, 6.0, ((0, 4), (1, 4), (2, 16)))
    response = scatter_about(streams_of[1], (N_LAYER, ORDER // N_LAYER, ORDER), (ORDER // 4) ** -0.5, 0.125, ((0, 4), (1, 4), (2, 16)))
    density_mask = with_ends((jax.random.randint(streams_of[2], (NBLK, N_LAYER, NBLK // N_LAYER), 0, 2) < 1).astype(jnp.int32), jax.random.fold_in(streams_of[2], 1), 0, 1)
    response_mask = with_ends((jax.random.randint(streams_of[3], (N_LAYER, NBLK // N_LAYER, NBLK), 0, 2) < 1).astype(jnp.int32), jax.random.fold_in(streams_of[3], 1), 0, 1)
    result_mask = with_ends((jax.random.randint(streams_of[4], (NBLK, NBLK), 0, 2) < 1).astype(jnp.int32), jax.random.fold_in(streams_of[4], 1), 0, 1)
    return {"density": density, "response": response, "density_mask": density_mask, "response_mask": response_mask, "result_mask": result_mask}


def expand_mask(values, pattern):
    height, breadth = values.shape
    block_rows, block_cols = pattern.shape
    shaped = values.reshape(block_rows, height // block_rows, block_cols, breadth // block_cols)
    masked = shaped * pattern[:, None, :, None].astype(values.dtype)
    return masked.reshape(height, breadth)


def reference(density, response, density_mask, response_mask, result_mask):
    left = expand_mask(density.reshape(ORDER, ORDER), density_mask.reshape(NBLK, NBLK))
    right = expand_mask(response.reshape(ORDER, ORDER), response_mask.reshape(NBLK, NBLK))
    product = jnp.dot(left, right, preferred_element_type=jnp.float32)
    product = expand_mask(product, result_mask).astype(jnp.bfloat16)
    widened = product.astype(jnp.float32)
    summed = (widened + widened.T).astype(jnp.bfloat16)
    return summed.reshape(BANDS, N_COL, SLAB, ORDER)
```

```python
import jax
import jax.numpy as jnp
from jax import lax
from jax.experimental import pallas as pl
from jax.experimental.pallas import tpu as pltpu
from jax.sharding import PartitionSpec as P

NQ = 4
MQ = 2048 // NQ
TAIL = 16
BF = jnp.bfloat16
F32 = jnp.float32
VMEM = pltpu.VMEM
WHOLE = pl.BlockSpec(memory_space=pltpu.VMEM)
SCALARS = pl.BlockSpec(memory_space=pltpu.SMEM)
ANYWHERE = pl.BlockSpec(memory_space=pl.ANY)


def params(mib=48):
    return pltpu.CompilerParams(vmem_limit_bytes=mib * 1024 * 1024)


def cost(flops, moved):
    return pl.CostEstimate(flops=flops, bytes_accessed=moved, transcendentals=0)


def position():
    place = lax.axis_index("col")
    return lax.axis_index("row"), place // 2, place % 2, lax.axis_index("layer")


def rows_of(q):
    return MQ + TAIL if q == 0 else MQ


def prep_a_kernel(dm, a, rm, *rest):
    outs, spare = rest[:NQ], rest[NQ]
    per = 4 // NQ
    for q in range(NQ):
        for xb in range(4):
            for j in range(per):
                block = xb * 4 + q * per + j
                keep = dm[block].astype(F32)
                value = a[block * 128 : (block + 1) * 128, :].astype(F32) * keep
                at = (xb * per + j) * 128
                outs[q][at : at + 128, :] = value.astype(BF)
    spare[...] = jnp.zeros_like(spare)
    spare[0:4, 0:16] = rm[...].astype(F32)
    outs[0][MQ : MQ + TAIL, :] = spare[...].astype(BF)


def prep_a(a, dm, rm):
    return pl.pallas_call(
        prep_a_kernel,
        out_shape=[jax.ShapeDtypeStruct((rows_of(q), 128), BF) for q in range(NQ)],
        in_specs=[SCALARS, WHOLE, WHOLE],
        out_specs=[WHOLE] * NQ,
        scratch_shapes=[VMEM((TAIL, 128), F32)],
        compiler_params=params(),
        cost_estimate=cost(2048 * 128, 2 * 2048 * 128 * 2),
    )(dm, a, rm)


def prep_b_kernel(mask, b, out):
    for tb in range(4):
        for cb in range(4):
            keep = mask[tb, cb].astype(F32)
            block = b[tb * 128 : (tb + 1) * 128, cb * 128 : (cb + 1) * 128].astype(F32) * keep
            flipped = block.T.astype(BF)
            lanes = slice((tb // 2) * 128, (tb // 2 + 1) * 128)
            for e in range(2):
                out[(2 * cb + e) * 2 + tb % 2, :, lanes] = flipped[e * 64 : (e + 1) * 64, :]


def prep_b(b, mask):
    return pl.pallas_call(
        prep_b_kernel,
        out_shape=jax.ShapeDtypeStruct((16, 64, 256), BF),
        in_specs=[SCALARS, WHOLE],
        out_specs=WHOLE,
        compiler_params=params(),
        cost_estimate=cost(512 * 512, 2 * 512 * 512 * 2),
    )(mask, b)


def load_and_multiply(q, half, pieces, bs, a_full, b_full, sems, tails):
    y, z, core, _ = position()
    copies = []
    for s in range(4):
        y0 = lax.rem(y - s + 4, 4)
        copies.append(pltpu.make_async_copy(bs[s].at[:, half], b_full.at[y0], sems.at[8 + s]))
    for s in range(8):
        z0 = lax.rem(z - s + 8, 8)
        lanes = pl.ds(pl.multiple_of(z0 * 128, 128), 128)
        copies.append(pltpu.make_async_copy(pieces[s].at[0:MQ], a_full.at[:, lanes], sems.at[s]))
    if q == 0:
        for s in range(8):
            copies.append(pltpu.make_async_copy(pieces[s].at[MQ : MQ + TAIL], tails.at[s], sems.at[12 + s]))
    for copy in copies:
        copy.start()
    for copy in copies:
        copy.wait()
    total = None
    for y0 in range(4):
        term = lax.dot_general(
            a_full[:, y0 * 256 : (y0 + 1) * 256],
            b_full[y0].reshape(512, 256),
            (((1,), (1,)), ((), ())),
            preferred_element_type=F32,
        )
        total = term if total is None else total + term
    return total


def mask_rows(tails):
    _, z, core, _ = position()
    row = lax.broadcasted_iota(jnp.int32, (TAIL, 128), 0)
    lane = lax.broadcasted_iota(jnp.int32, (TAIL, 128), 1)
    wide = lax.broadcasted_iota(jnp.int32, (TAIL, 512), 1) // 32
    mask = jnp.zeros((TAIL, 512), F32)
    for s in range(8):
        z0 = lax.rem(z - s + 8, 8)
        values = tails[s].astype(F32)
        chosen = jnp.sum(jnp.where(row == z // 2, values, 0.0), axis=0, keepdims=True)
        column = jnp.sum(jnp.where(row == lane, chosen, 0.0), axis=1, keepdims=True)
        mask = jnp.where(wide == 2 * z0 + core, column, mask)
    return mask


def send_kernel(q, *refs):
    pieces, bs, out = refs[:8], refs[8:12], refs[12]
    a_full, b_full, tails, sems = refs[13:]
    core = position()[2]
    total = load_and_multiply(q, 1 - core, pieces, bs, a_full, b_full, sems, tails)
    out[0:MQ, :] = total.astype(BF)
    if q == 0:
        out[MQ : MQ + TAIL, :] = mask_rows(tails).astype(BF)


def scratches():
    return [
        VMEM((MQ, 1024), BF),
        VMEM((4, 16, 32, 256), BF),
        VMEM((8, TAIL, 128), BF),
        pltpu.SemaphoreType.DMA((20,)),
    ]


def send_half(q, pieces, bs):
    return pl.pallas_call(
        lambda *refs: send_kernel(q, *refs),
        out_shape=jax.ShapeDtypeStruct((rows_of(q), 512), BF),
        in_specs=[ANYWHERE] * 12,
        out_specs=WHOLE,
        scratch_shapes=scratches(),
        compiler_params=params(),
        cost_estimate=cost(2 * MQ * 1024 * 512, MQ * 1024 * 2 + 1024 * 1024),
    )(*pieces, *bs)


def keep_kernel(q, *refs):
    pieces, bs, received = refs[:8], refs[8:12], refs[12]
    own, outs = refs[13], refs[14:17]
    rest = refs[17:]
    if q == 0:
        mask, rest = rest[0], rest[1:]
    a_full, b_full, tails, sems, total = rest
    _, _, core, x = position()
    part = load_and_multiply(q, core, pieces, bs, a_full, b_full, sems, tails)
    total[...] = (part + received[0:MQ, :].astype(F32)).reshape(4, MQ // 4, 512)
    own[...] = total[x]
    for s in range(1, 4):
        outs[s - 1][...] = total[lax.rem(x + s, 4)].astype(BF)
    if q == 0:
        mask[...] = mask_rows(tails) + received[MQ : MQ + TAIL, :].astype(F32)


def keep_half(q, pieces, bs, received):
    part = (MQ // 4, 512)
    shapes = [jax.ShapeDtypeStruct(part, F32)] + [jax.ShapeDtypeStruct(part, BF)] * 3
    if q == 0:
        shapes.append(jax.ShapeDtypeStruct((TAIL, 512), F32))
    return pl.pallas_call(
        lambda *refs: keep_kernel(q, *refs),
        out_shape=shapes,
        in_specs=[ANYWHERE] * 12 + [WHOLE],
        out_specs=[WHOLE] * len(shapes),
        scratch_shapes=scratches() + [VMEM((4, MQ // 4, 512), F32)],
        compiler_params=params(),
        cost_estimate=cost(2 * MQ * 1024 * 512, MQ * 1024 * 2 + 2 * 1024 * 1024),
    )(*pieces, *bs, received)


def sum_kernel(*refs):
    mask, parts, out, flipped = refs[0], refs[1:-2], refs[-2], refs[-1]
    x = position()[3]
    for q in range(NQ):
        own, first, second, third = parts[4 * q : 4 * q + 4]
        for j in range(4 // NQ):
            block = q * (4 // NQ) + j
            rows = slice(j * 128, (j + 1) * 128)
            value = own[rows, :] + first[rows, :].astype(F32) + second[rows, :].astype(F32) + third[rows, :].astype(F32)
            value = value * mask[pl.ds(x * 4 + block, 1), :]
            out[block * 128 : (block + 1) * 128, :] = value.astype(BF)
            flipped[:, block * 128 : (block + 1) * 128] = value.T.astype(BF)


def sum_parts(mask, parts):
    return pl.pallas_call(
        sum_kernel,
        out_shape=[jax.ShapeDtypeStruct((512, 512), BF)] * 2,
        in_specs=[WHOLE] * (1 + len(parts)),
        out_specs=[WHOLE] * 2,
        compiler_params=params(),
        cost_estimate=cost(512 * 512 * 5, 512 * 512 * 14),
    )(mask, *parts)


def final_kernel(own, mirrored, out):
    group = lax.broadcasted_iota(jnp.int32, (32, 128), 1) // 32
    for k_high in range(4):
        for b_high in range(4):
            sources = [own[4 * k_high + k, :, b_high * 128 : (b_high + 1) * 128].astype(F32) for k in range(4)]
            for b in range(4):
                value = None
                for k in range(4):
                    shift = ((k - b) % 4) * 32
                    turned = pltpu.roll(sources[k], shift, 1) if shift else sources[k]
                    value = turned if value is None else jnp.where(group == k, turned, value)
                band = b_high * 4 + b
                value = value + mirrored[band, :, k_high * 128 : (k_high + 1) * 128].astype(F32)
                at = band * 512 + k_high * 128
                out[:, at : at + 128] = value.astype(BF)


def finish(own, mirrored):
    return pl.pallas_call(
        final_kernel,
        out_shape=jax.ShapeDtypeStruct((32, 8192), BF),
        in_specs=[WHOLE] * 2,
        out_specs=WHOLE,
        compiler_params=params(),
        cost_estimate=cost(32 * 8192 * 8, 3 * 32 * 8192 * 2),
    )(own, mirrored)


def turn_z(value, shift):
    pairs = [(2 * z + c, 2 * ((z + shift) % 8) + c) for z in range(8) for c in range(2)]
    return lax.ppermute(value, "col", pairs)


def turn(value, axis, shift):
    return lax.ppermute(value, axis, [(i, (i + shift) % 4) for i in range(4)])


def per_device(density, response, density_mask, response_mask, result_mask):
    b_send = prep_b(response.reshape(512, 512), response_mask.reshape(4, 4))
    chunks = prep_a(density.reshape(2048, 128), density_mask.reshape(16), result_mask.T)

    b_own = lax.all_to_all(b_send, "col", 0, 0)
    bs = [b_own] + [turn(b_own, "row", s) for s in (1, 2, 3)]
    bs = [value.reshape(16, 2, 32, 256) for value in bs]

    gathered = [{0: chunk} for chunk in chunks]
    for step in range(1, 5):
        for q in range(NQ):
            got = gathered[q]
            if step < 4 or q % 2 == 0:
                got[step] = turn_z(got[step - 1], 1)
            if step < 4 or q % 2 == 1:
                got[8 - step] = turn_z(got[(9 - step) % 8], -1)

    parts = []
    mask = None
    for q in range(NQ):
        pieces = [gathered[q][s] for s in range(8)]
        other = send_half(q, pieces, bs)
        received = lax.ppermute(other, "col", [(i, i ^ 1) for i in range(16)])
        kept = keep_half(q, pieces, bs, received)
        if q == 0:
            mask = kept[4]
        parts += [kept[0]] + [turn(kept[s], "layer", s) for s in (1, 2, 3)]

    product, flipped = sum_parts(mask, parts)
    own = lax.all_to_all(product.reshape(16, 32, 512), "col", 0, 0)
    mirrored = lax.all_to_all(flipped.reshape(16, 32, 512), ("row", "layer"), 0, 0)
    return finish(own, mirrored).reshape(1, 1, 32, 8192)


def solution(mesh):
    placed = (
        P("row", "layer", "col"),
        P("layer", "row", "col"),
        P("row", "layer", "col"),
        P("layer", "row", "col"),
        P("row", "col"),
    )
    return jax.shard_map(
        per_device,
        mesh=mesh,
        in_specs=placed,
        out_specs=P(("row", "layer"), "col", None, None),
        check_vma=False,
    )
```

```python
import jax
import jax.numpy as jnp
from jax import lax
from jax.experimental import pallas as pl
from jax.experimental.pallas import tpu as pltpu
from jax.sharding import PartitionSpec as P

NQ = 2
MQ = 2048 // NQ
TAIL = 16
BF = jnp.bfloat16
F32 = jnp.float32
VMEM = pltpu.VMEM
WHOLE = pl.BlockSpec(memory_space=pltpu.VMEM)
SCALARS = pl.BlockSpec(memory_space=pltpu.SMEM)
ANYWHERE = pl.BlockSpec(memory_space=pl.ANY)


def params(mib=48):
    return pltpu.CompilerParams(vmem_limit_bytes=mib * 1024 * 1024)


def cost(flops, moved):
    return pl.CostEstimate(flops=flops, bytes_accessed=moved, transcendentals=0)


def position():
    place = lax.axis_index("col")
    return lax.axis_index("row"), place // 2, place % 2, lax.axis_index("layer")


def rows_of(q):
    return MQ + TAIL if q == 0 else MQ


def prep_a_kernel(dm, a, rm, *rest):
    outs, spare = rest[:NQ], rest[NQ]
    per = 4 // NQ
    for q in range(NQ):
        for xb in range(4):
            for j in range(per):
                block = xb * 4 + q * per + j
                keep = dm[block].astype(F32)
                value = a[block * 128 : (block + 1) * 128, :].astype(F32) * keep
                at = (xb * per + j) * 128
                outs[q][at : at + 128, :] = value.astype(BF)
    spare[...] = jnp.zeros_like(spare)
    spare[0:4, 0:16] = rm[...].astype(F32)
    outs[0][MQ : MQ + TAIL, :] = spare[...].astype(BF)


def prep_a(a, dm, rm):
    return pl.pallas_call(
        prep_a_kernel,
        out_shape=[jax.ShapeDtypeStruct((rows_of(q), 128), BF) for q in range(NQ)],
        in_specs=[SCALARS, WHOLE, WHOLE],
        out_specs=[WHOLE] * NQ,
        scratch_shapes=[VMEM((TAIL, 128), F32)],
        compiler_params=params(),
        cost_estimate=cost(2048 * 128, 2 * 2048 * 128 * 2),
    )(dm, a, rm)


def prep_b_kernel(mask, b, out):
    for tb in range(4):
        for cb in range(4):
            keep = mask[tb, cb].astype(F32)
            block = b[tb * 128 : (tb + 1) * 128, cb * 128 : (cb + 1) * 128].astype(F32) * keep
            flipped = block.T.astype(BF)
            lanes = slice((tb // 2) * 128, (tb // 2 + 1) * 128)
            for e in range(2):
                out[(2 * cb + e) * 2 + tb % 2, :, lanes] = flipped[e * 64 : (e + 1) * 64, :]


def prep_b(b, mask):
    return pl.pallas_call(
        prep_b_kernel,
        out_shape=jax.ShapeDtypeStruct((16, 64, 256), BF),
        in_specs=[SCALARS, WHOLE],
        out_specs=WHOLE,
        compiler_params=params(),
        cost_estimate=cost(512 * 512, 2 * 512 * 512 * 2),
    )(mask, b)


def load_and_multiply(q, half, pieces, bs, a_full, b_full, sems, tails):
    y, z, core, _ = position()
    copies = []
    bands = (slice(0, 16), slice(0, 16), slice(0, 16), slice(0, 8), slice(8, 16))
    for s, back in enumerate((0, 1, 3, 2, 2)):
        y0 = lax.rem(y - back + 4, 4)
        copies.append(pltpu.make_async_copy(bs[s].at[:, half], b_full.at[y0, bands[s]], sems.at[8 + s]))
    for s in range(8):
        z0 = lax.rem(z - s + 8, 8)
        lanes = pl.ds(pl.multiple_of(z0 * 128, 128), 128)
        copies.append(pltpu.make_async_copy(pieces[s].at[0:MQ], a_full.at[:, lanes], sems.at[s]))
    if q == 0:
        for s in range(8):
            copies.append(pltpu.make_async_copy(pieces[s].at[MQ : MQ + TAIL], tails.at[s], sems.at[13 + s]))
    for copy in copies:
        copy.start()
    for copy in copies:
        copy.wait()
    total = None
    for y0 in range(4):
        term = lax.dot_general(
            a_full[:, y0 * 256 : (y0 + 1) * 256],
            b_full[y0].reshape(512, 256),
            (((1,), (1,)), ((), ())),
            preferred_element_type=F32,
        )
        total = term if total is None else total + term
    return total


def mask_rows(tails):
    _, z, core, _ = position()
    row = lax.broadcasted_iota(jnp.int32, (TAIL, 128), 0)
    lane = lax.broadcasted_iota(jnp.int32, (TAIL, 128), 1)
    wide = lax.broadcasted_iota(jnp.int32, (TAIL, 512), 1) // 32
    mask = jnp.zeros((TAIL, 512), F32)
    for s in range(8):
        z0 = lax.rem(z - s + 8, 8)
        values = tails[s].astype(F32)
        chosen = jnp.sum(jnp.where(row == z // 2, values, 0.0), axis=0, keepdims=True)
        column = jnp.sum(jnp.where(row == lane, chosen, 0.0), axis=1, keepdims=True)
        mask = jnp.where(wide == 2 * z0 + core, column, mask)
    return mask


def send_kernel(q, *refs):
    pieces, bs, out = refs[:8], refs[8:13], refs[13]
    a_full, b_full, tails, sems = refs[14:]
    core = position()[2]
    total = load_and_multiply(q, 1 - core, pieces, bs, a_full, b_full, sems, tails)
    out[0:MQ, :] = total.astype(BF)
    if q == 0:
        out[MQ : MQ + TAIL, :] = mask_rows(tails).astype(BF)


def scratches():
    return [
        VMEM((MQ, 1024), BF),
        VMEM((4, 16, 32, 256), BF),
        VMEM((8, TAIL, 128), BF),
        pltpu.SemaphoreType.DMA((21,)),
    ]


def send_half(q, pieces, bs):
    return pl.pallas_call(
        lambda *refs: send_kernel(q, *refs),
        out_shape=jax.ShapeDtypeStruct((rows_of(q), 512), BF),
        in_specs=[ANYWHERE] * 13,
        out_specs=WHOLE,
        scratch_shapes=scratches(),
        compiler_params=params(),
        cost_estimate=cost(2 * MQ * 1024 * 512, MQ * 1024 * 2 + 1024 * 1024),
    )(*pieces, *bs)


def keep_kernel(q, *refs):
    pieces, bs, received = refs[:8], refs[8:13], refs[13]
    own, outs = refs[14], refs[15:18]
    rest = refs[18:]
    if q == 0:
        mask, rest = rest[0], rest[1:]
    a_full, b_full, tails, sems, total = rest
    _, _, core, x = position()
    part = load_and_multiply(q, core, pieces, bs, a_full, b_full, sems, tails)
    total[...] = (part + received[0:MQ, :].astype(F32)).reshape(4, MQ // 4, 512)
    own[...] = total[x]
    for s in range(1, 4):
        outs[s - 1][...] = total[lax.rem(x + s, 4)].astype(BF)
    if q == 0:
        mask[...] = mask_rows(tails) + received[MQ : MQ + TAIL, :].astype(F32)


def keep_half(q, pieces, bs, received):
    part = (MQ // 4, 512)
    shapes = [jax.ShapeDtypeStruct(part, F32)] + [jax.ShapeDtypeStruct(part, BF)] * 3
    if q == 0:
        shapes.append(jax.ShapeDtypeStruct((TAIL, 512), F32))
    return pl.pallas_call(
        lambda *refs: keep_kernel(q, *refs),
        out_shape=shapes,
        in_specs=[ANYWHERE] * 13 + [WHOLE],
        out_specs=[WHOLE] * len(shapes),
        scratch_shapes=scratches() + [VMEM((4, MQ // 4, 512), F32)],
        compiler_params=params(),
        cost_estimate=cost(2 * MQ * 1024 * 512, MQ * 1024 * 2 + 2 * 1024 * 1024),
    )(*pieces, *bs, received)


def sum_kernel(*refs):
    mask, parts, out, flipped = refs[0], refs[1:-2], refs[-2], refs[-1]
    x = position()[3]
    for q in range(NQ):
        own, first, second, third = parts[4 * q : 4 * q + 4]
        for j in range(4 // NQ):
            block = q * (4 // NQ) + j
            rows = slice(j * 128, (j + 1) * 128)
            value = own[rows, :] + first[rows, :].astype(F32) + second[rows, :].astype(F32) + third[rows, :].astype(F32)
            value = value * mask[pl.ds(x * 4 + block, 1), :]
            out[block * 128 : (block + 1) * 128, :] = value.astype(BF)
            flipped[:, block * 128 : (block + 1) * 128] = value.T.astype(BF)


def sum_parts(mask, parts):
    return pl.pallas_call(
        sum_kernel,
        out_shape=[jax.ShapeDtypeStruct((512, 512), BF)] * 2,
        in_specs=[WHOLE] * (1 + len(parts)),
        out_specs=[WHOLE] * 2,
        compiler_params=params(),
        cost_estimate=cost(512 * 512 * 5, 512 * 512 * 14),
    )(mask, *parts)


def final_kernel(own, mirrored, out):
    group = lax.broadcasted_iota(jnp.int32, (32, 128), 1) // 32
    for k_high in range(4):
        for b_high in range(4):
            sources = [own[4 * k_high + k, :, b_high * 128 : (b_high + 1) * 128].astype(F32) for k in range(4)]
            for b in range(4):
                value = None
                for k in range(4):
                    shift = ((k - b) % 4) * 32
                    turned = pltpu.roll(sources[k], shift, 1) if shift else sources[k]
                    value = turned if value is None else jnp.where(group == k, turned, value)
                band = b_high * 4 + b
                value = value + mirrored[band, :, k_high * 128 : (k_high + 1) * 128].astype(F32)
                at = band * 512 + k_high * 128
                out[:, at : at + 128] = value.astype(BF)


def finish(own, mirrored):
    return pl.pallas_call(
        final_kernel,
        out_shape=jax.ShapeDtypeStruct((32, 8192), BF),
        in_specs=[WHOLE] * 2,
        out_specs=WHOLE,
        compiler_params=params(),
        cost_estimate=cost(32 * 8192 * 8, 3 * 32 * 8192 * 2),
    )(own, mirrored)


def turn_z(value, shift):
    pairs = [(2 * z + c, 2 * ((z + shift) % 8) + c) for z in range(8) for c in range(2)]
    return lax.ppermute(value, "col", pairs)


def turn(value, axis, shift):
    return lax.ppermute(value, axis, [(i, (i + shift) % 4) for i in range(4)])


def per_device(density, response, density_mask, response_mask, result_mask):
    chunks = prep_a(density.reshape(2048, 128), density_mask.reshape(16), result_mask.T)
    chunks, response = lax.optimization_barrier((chunks, response))
    b_send = prep_b(response.reshape(512, 512), response_mask.reshape(4, 4))

    b_own = lax.all_to_all(b_send, "col", 0, 0)
    behind, ahead = turn(b_own, "row", 1), turn(b_own, "row", -1)
    bs = [b_own, behind, ahead, turn(behind[:8], "row", 1), turn(ahead[8:], "row", -1)]
    bs = [value.reshape(-1, 2, 32, 256) for value in bs]

    gathered = [{0: chunk} for chunk in chunks]
    for step in range(1, 5):
        for q in range(NQ):
            got = gathered[q]
            if step < 4 or q % 2 == 0:
                got[step] = turn_z(got[step - 1], 1)
            if step < 4 or q % 2 == 1:
                got[8 - step] = turn_z(got[(9 - step) % 8], -1)

    parts = []
    mask = None
    for q in range(NQ):
        pieces = [gathered[q][s] for s in range(8)]
        other = send_half(q, pieces, bs)
        received = lax.ppermute(other, "col", [(i, i ^ 1) for i in range(16)])
        kept = keep_half(q, pieces, bs, received)
        if q == 0:
            mask = kept[4]
        parts += [kept[0]] + [turn(kept[s], "layer", s) for s in (1, 2, 3)]

    product, flipped = sum_parts(mask, parts)
    own = lax.all_to_all(product.reshape(16, 32, 512), "col", 0, 0)
    mirrored = lax.all_to_all(flipped.reshape(16, 32, 512), ("row", "layer"), 0, 0)
    return finish(own, mirrored).reshape(1, 1, 32, 8192)


def solution(mesh):
    placed = (
        P("row", "layer", "col"),
        P("layer", "row", "col"),
        P("row", "layer", "col"),
        P("layer", "row", "col"),
        P("row", "col"),
    )
    return jax.shard_map(
        per_device,
        mesh=mesh,
        in_specs=placed,
        out_specs=P(("row", "layer"), "col", None, None),
        check_vma=False,
    )
```

```python
import jax
import jax.numpy as jnp
from jax import lax
from jax.experimental import pallas as pl
from jax.experimental.pallas import tpu as pltpu
from jax.sharding import PartitionSpec as P

NQ = 2
MQ = 2048 // NQ
TAIL = 16
BF = jnp.bfloat16
F32 = jnp.float32
VMEM = pltpu.VMEM
WHOLE = pl.BlockSpec(memory_space=pltpu.VMEM)
SCALARS = pl.BlockSpec(memory_space=pltpu.SMEM)
ANYWHERE = pl.BlockSpec(memory_space=pl.ANY)


def params(mib=16):
    return pltpu.CompilerParams(vmem_limit_bytes=mib * 1024 * 1024)


def cost(flops, moved):
    return pl.CostEstimate(flops=flops, bytes_accessed=moved, transcendentals=0)


def position():
    place = lax.axis_index("col")
    return lax.axis_index("row"), place // 2, place % 2, lax.axis_index("layer")


def rows_of(q):
    return MQ + TAIL if q == 0 else MQ


def prep_a_kernel(dm, a, rm, *rest):
    outs, spare = rest[:NQ], rest[NQ]
    per = 4 // NQ
    for q in range(NQ):
        for xb in range(4):
            for j in range(per):
                block = xb * 4 + q * per + j
                keep = dm[block].astype(F32)
                value = a[block * 128 : (block + 1) * 128, :].astype(F32) * keep
                at = (xb * per + j) * 128
                outs[q][at : at + 128, :] = value.astype(BF)
    spare[...] = jnp.zeros_like(spare)
    spare[0:4, 0:16] = rm[...].astype(F32)
    outs[0][MQ : MQ + TAIL, :] = spare[...].astype(BF)


def prep_a(a, dm, rm):
    return pl.pallas_call(
        prep_a_kernel,
        out_shape=[jax.ShapeDtypeStruct((rows_of(q), 128), BF) for q in range(NQ)],
        in_specs=[SCALARS, WHOLE, WHOLE],
        out_specs=[WHOLE] * NQ,
        scratch_shapes=[VMEM((TAIL, 128), F32)],
        compiler_params=params(),
        cost_estimate=cost(2048 * 128, 2 * 2048 * 128 * 2),
    )(dm, a, rm)


def prep_b_kernel(mask, b, out):
    for tb in range(4):
        for cb in range(4):
            keep = mask[tb, cb].astype(F32)
            block = b[tb * 128 : (tb + 1) * 128, cb * 128 : (cb + 1) * 128].astype(F32) * keep
            flipped = block.T.astype(BF)
            lanes = slice((tb // 2) * 128, (tb // 2 + 1) * 128)
            for e in range(2):
                out[(2 * cb + e) * 2 + tb % 2, :, lanes] = flipped[e * 64 : (e + 1) * 64, :]


def prep_b(b, mask):
    return pl.pallas_call(
        prep_b_kernel,
        out_shape=jax.ShapeDtypeStruct((16, 64, 256), BF),
        in_specs=[SCALARS, WHOLE],
        out_specs=WHOLE,
        compiler_params=params(),
        cost_estimate=cost(512 * 512, 2 * 512 * 512 * 2),
    )(mask, b)


def load(q, half, pieces, bs, a_full, b_full, sems, b_sems, tails, more=()):
    y, z, _, x = position()
    copies = list(more)
    bands = (slice(0, 4), slice(0, 4), slice(0, 4), slice(0, 2), slice(2, 4))
    for s, back in enumerate((0, 1, 3, 2, 2)):
        lanes = pl.ds(pl.multiple_of(lax.rem(y - back + 4, 4) * 256, 256), 256)
        for ahead in range(4):
            layer = lax.rem(x + ahead, 4)
            to = b_full.at[ahead, bands[s], :, lanes]
            copies.append(pltpu.make_async_copy(bs[s].at[:, layer, half], to, b_sems.at[4 * s + ahead]))
    for s in range(8):
        lanes = pl.ds(pl.multiple_of(lax.rem(z - s + 8, 8) * 128, 128), 128)
        copies.append(pltpu.make_async_copy(pieces[s].at[0:MQ], a_full.at[:, lanes], sems.at[s]))
    if q == 0:
        for s in range(8):
            copies.append(pltpu.make_async_copy(pieces[s].at[MQ : MQ + TAIL], tails.at[s], sems.at[13 + s]))
    for copy in copies:
        copy.start()
    for copy in copies:
        copy.wait()


def multiply(a_full, b_full, rows):
    return lax.dot_general(
        a_full[rows, :],
        b_full[...].reshape(512, 1024),
        (((1,), (1,)), ((), ())),
        preferred_element_type=F32,
    )


def mask_rows(tails):
    _, z, core, x = position()
    row = lax.broadcasted_iota(jnp.int32, (TAIL, 128), 0)
    lane = lax.broadcasted_iota(jnp.int32, (TAIL, 128), 1)
    mask = jnp.zeros((TAIL, 128), F32)
    for s in range(8):
        band = 2 * lax.rem(z - s + 8, 8) + core
        values = tails[s].astype(F32)
        chosen = jnp.sum(jnp.where(row == z // 2, values, 0.0), axis=0, keepdims=True)
        column = jnp.sum(jnp.where(row == lane, chosen, 0.0), axis=1, keepdims=True)
        mask = jnp.where(lane // 32 * 4 + x == band, column, mask)
    return mask


def send_kernel(q, *refs):
    pieces, bs, out = refs[:8], refs[8:13], refs[13]
    a_full, b_full, tails, sems, b_sems = refs[14:]
    core = position()[2]
    load(q, 1 - core, pieces, bs, a_full, b_full, sems, b_sems, tails)
    for part in range(4):
        rows = slice(part * (MQ // 4), (part + 1) * (MQ // 4))
        out[rows, :] = multiply(a_full, b_full, rows).astype(BF)
    if q == 0:
        out[MQ : MQ + TAIL, :] = jnp.zeros((TAIL, 512), BF)
        out[MQ : MQ + TAIL, 0:128] = mask_rows(tails).astype(BF)


def scratches():
    return [
        VMEM((MQ, 1024), BF),
        VMEM((4, 4, 32, 1024), BF),
        VMEM((8, TAIL, 128), BF),
        pltpu.SemaphoreType.DMA((22,)),
        pltpu.SemaphoreType.DMA((20,)),
    ]


def send_half(q, pieces, bs):
    return pl.pallas_call(
        lambda *refs: send_kernel(q, *refs),
        out_shape=jax.ShapeDtypeStruct((rows_of(q), 512), BF),
        in_specs=[ANYWHERE] * 13,
        out_specs=WHOLE,
        scratch_shapes=scratches(),
        compiler_params=params(),
        cost_estimate=cost(2 * MQ * 1024 * 512, MQ * 1024 * 2 + 1024 * 1024),
    )(*pieces, *bs)


def keep_kernel(q, *refs):
    pieces, bs, received = refs[:8], refs[8:13], refs[13]
    own, outs = refs[14], refs[15:18]
    rest = refs[18:]
    if q == 0:
        mask, rest = rest[0], rest[1:]
    a_full, b_full, tails, sems, b_sems, other = rest
    core = position()[2]
    arrival = pltpu.make_async_copy(received, other, sems.at[21])
    load(q, core, pieces, bs, a_full, b_full, sems, b_sems, tails, [arrival])
    for part in range(4):
        rows = slice(part * (MQ // 4), (part + 1) * (MQ // 4))
        value = multiply(a_full, b_full, rows) + other[rows, :].astype(F32)
        own[rows, :] = value[:, 0:128]
        for s in range(1, 4):
            outs[s - 1][rows, :] = value[:, s * 128 : (s + 1) * 128].astype(BF)
    if q == 0:
        mask[...] = mask_rows(tails) + other[MQ : MQ + TAIL, 0:128].astype(F32)


def keep_half(q, pieces, bs, received):
    part = (MQ, 128)
    shapes = [jax.ShapeDtypeStruct(part, F32)] + [jax.ShapeDtypeStruct(part, BF)] * 3
    if q == 0:
        shapes.append(jax.ShapeDtypeStruct((TAIL, 128), F32))
    return pl.pallas_call(
        lambda *refs: keep_kernel(q, *refs),
        out_shape=shapes,
        in_specs=[ANYWHERE] * 14,
        out_specs=[WHOLE] * len(shapes),
        scratch_shapes=scratches() + [VMEM((rows_of(q), 512), BF)],
        compiler_params=params(),
        cost_estimate=cost(2 * MQ * 1024 * 512, MQ * 1024 * 2 + 2 * 1024 * 1024),
    )(*pieces, *bs, received)


def sum_kernel(*refs):
    mask, parts, out, flips, turned = refs[0], refs[1:-6], refs[-6], refs[-5:-1], refs[-1]
    y = position()[0]
    size = MQ // 4
    for xb in range(4):
        for q in range(NQ):
            own, first, second, third = parts[4 * q : 4 * q + 4]
            for j in range(4 // NQ):
                at = xb * size + j * 128
                rows = slice(at, at + 128)
                value = own[rows, :] + first[rows, :].astype(F32)
                value = value + second[rows, :].astype(F32) + third[rows, :].astype(F32)
                block = q * (4 // NQ) + j
                value = value * mask[xb * 4 + block : xb * 4 + block + 1, :]
                out[4 * block : 4 * block + 4, xb] = value.astype(BF).reshape(4, 32, 128)
                lanes = slice((xb * 4 + block) * 128, (xb * 4 + block + 1) * 128)
                turned[:, :, lanes] = value.T.astype(BF).reshape(4, 32, 128)
    for s in range(4):
        flips[s][...] = turned[lax.rem(y + s, 4)]


def sum_parts(mask, parts):
    return pl.pallas_call(
        sum_kernel,
        out_shape=[jax.ShapeDtypeStruct((16, 4, 32, 128), BF)] + [jax.ShapeDtypeStruct((32, 2048), BF)] * 4,
        in_specs=[WHOLE] * (1 + len(parts)),
        out_specs=[WHOLE] * 5,
        scratch_shapes=[VMEM((4, 32, 2048), BF)],
        compiler_params=params(),
        cost_estimate=cost(512 * 512 * 5, 512 * 512 * 14),
    )(mask, *parts)


def final_kernel(own, *refs):
    mirrored, out, ordered = refs[:4], refs[4], refs[5]
    y = position()[0]
    for s in range(4):
        ordered[lax.rem(y - s + 4, 4)] = mirrored[s][...]
    group = lax.broadcasted_iota(jnp.int32, (32, 128), 1) // 32
    for k_high in range(4):
        for layer in range(4):
            sources = [own[(4 * k_high + k) * 4 + layer].astype(F32) for k in range(4)]
            at = layer * 512 + k_high * 128
            for row in range(4):
                value = None
                for k in range(4):
                    shift = ((k - row) % 4) * 32
                    turned = pltpu.roll(sources[k], shift, 1) if shift else sources[k]
                    value = turned if value is None else jnp.where(group == k, turned, value)
                value = value + ordered[row, :, at : at + 128].astype(F32)
                out[:, row * 2048 + at : row * 2048 + at + 128] = value.astype(BF)


def finish(own, mirrored):
    return pl.pallas_call(
        final_kernel,
        out_shape=jax.ShapeDtypeStruct((32, 8192), BF),
        in_specs=[WHOLE] * 5,
        out_specs=WHOLE,
        scratch_shapes=[VMEM((4, 32, 2048), BF)],
        compiler_params=params(),
        cost_estimate=cost(32 * 8192 * 8, 3 * 32 * 8192 * 2),
    )(own, *mirrored)


def turn_z(value, shift):
    pairs = [(2 * z + c, 2 * ((z + shift) % 8) + c) for z in range(8) for c in range(2)]
    return lax.ppermute(value, "col", pairs)


def turn(value, axis, shift):
    return lax.ppermute(value, axis, [(i, (i + shift) % 4) for i in range(4)])


def per_device(density, response, density_mask, response_mask, result_mask):
    chunks = prep_a(density.reshape(2048, 128), density_mask.reshape(16), result_mask.T)
    chunks, response = lax.optimization_barrier((chunks, response))
    b_send = prep_b(response.reshape(512, 512), response_mask.reshape(4, 4))

    b_own = lax.all_to_all(b_send, "col", 0, 0)

    gathered = [{0: chunk} for chunk in chunks]
    for step in range(1, 5):
        if step == 2:
            gathered[1][1], gathered[1][7], b_own = lax.optimization_barrier((gathered[1][1], gathered[1][7], b_own))
        for q in range(NQ):
            got = gathered[q]
            if step < 4 or q % 2 == 0:
                got[step] = turn_z(got[step - 1], 1)
            if step < 4 or q % 2 == 1:
                got[8 - step] = turn_z(got[(9 - step) % 8], -1)

    behind, ahead = turn(b_own, "row", 1), turn(b_own, "row", -1)
    bs = [b_own, behind, ahead, turn(behind[:8], "row", 1), turn(ahead[8:], "row", -1)]
    bs = [value.reshape(-1, 4, 2, 32, 256) for value in bs]

    parts = []
    mask = None
    for q in range(NQ):
        pieces = [gathered[q][s] for s in range(8)]
        other = send_half(q, pieces, bs)
        received = lax.ppermute(other, "col", [(i, i ^ 1) for i in range(16)])
        kept = keep_half(q, pieces, bs, received)
        if q == 0:
            mask = kept[4]
        parts += [kept[0]] + [turn(kept[s], "layer", s) for s in (1, 2, 3)]

    product, *flips = sum_parts(mask, parts)
    own = lax.all_to_all(product.reshape(64, 32, 128), ("col", "layer"), 0, 0)
    mirrored = [flips[0]] + [turn(flips[s], "row", s) for s in (1, 2, 3)]
    return finish(own, mirrored).reshape(1, 1, 32, 8192)


def solution(mesh):
    placed = (
        P("row", "layer", "col"),
        P("layer", "row", "col"),
        P("row", "layer", "col"),
        P("layer", "row", "col"),
        P("row", "col"),
    )
    return jax.shard_map(
        per_device,
        mesh=mesh,
        in_specs=placed,
        out_specs=P(("row", "layer"), "col", None, None),
        check_vma=False,
    )
```

```python
import jax
import jax.numpy as jnp
from jax import lax
from jax.experimental import pallas as pl
from jax.experimental.pallas import tpu as pltpu
from jax.sharding import PartitionSpec as P

NQ = 2
MQ = 2048 // NQ
TAIL = 16
BF = jnp.bfloat16
F32 = jnp.float32
VMEM = pltpu.VMEM
WHOLE = pl.BlockSpec(memory_space=pltpu.VMEM)
FAR = pl.BlockSpec(memory_space=pltpu.HBM)
PREP = 60
ANYWHERE = pl.BlockSpec(memory_space=pl.ANY)


def params(mib=16):
    return pltpu.CompilerParams(vmem_limit_bytes=mib * 1024 * 1024)


def cost(flops, moved):
    return pl.CostEstimate(flops=flops, bytes_accessed=moved, transcendentals=0)


def position():
    place = lax.axis_index("col")
    return lax.axis_index("row"), place // 2, place % 2, lax.axis_index("layer")


def rows_of(q):
    return MQ + TAIL if q == 0 else MQ


def fetch(pairs, sems):
    copies = [pltpu.make_async_copy(source, to, sems.at[n]) for n, (source, to) in enumerate(pairs)]
    for copy in copies:
        copy.start()
    for copy in copies:
        copy.wait()


def prep_a_kernel(dm_in, a_in, rm_in, *rest):
    outs, (spare, dm, a, rm, sems) = rest[:NQ], rest[NQ:]
    fetch(((dm_in, dm), (a_in, a), (rm_in, rm)), sems)
    per = 4 // NQ
    for q in range(NQ):
        for xb in range(4):
            for j in range(per):
                block = xb * 4 + q * per + j
                keep = dm[0, block].astype(F32)
                value = a[block * 128 : (block + 1) * 128, :].astype(F32) * keep
                at = (xb * per + j) * 128
                outs[q][at : at + 128, :] = value.astype(BF)
    spare[...] = jnp.zeros_like(spare)
    spare[0:4, 0:16] = rm[...].astype(F32)
    outs[0][MQ : MQ + TAIL, :] = spare[...].astype(BF)


def prep_a(a, dm, rm):
    return pl.pallas_call(
        prep_a_kernel,
        out_shape=[jax.ShapeDtypeStruct((rows_of(q), 128), BF) for q in range(NQ)],
        in_specs=[FAR] * 3,
        out_specs=[WHOLE] * NQ,
        scratch_shapes=[
            VMEM((TAIL, 128), F32),
            pltpu.SMEM((1, 16), jnp.int32),
            VMEM((2048, 128), BF),
            VMEM((4, 16), jnp.int32),
            pltpu.SemaphoreType.DMA((3,)),
        ],
        compiler_params=params(PREP),
        cost_estimate=cost(2048 * 128, 2 * 2048 * 128 * 2),
    )(dm, a, rm)


def prep_b_kernel(mask_in, b_in, out, mask, b, sems):
    fetch(((mask_in, mask), (b_in, b)), sems)
    for tb in range(4):
        for cb in range(4):
            keep = mask[tb, cb].astype(F32)
            block = b[tb * 128 : (tb + 1) * 128, cb * 128 : (cb + 1) * 128].astype(F32) * keep
            flipped = block.T.astype(BF)
            lanes = slice((tb // 2) * 128, (tb // 2 + 1) * 128)
            for e in range(2):
                out[(2 * cb + e) * 2 + tb % 2, :, lanes] = flipped[e * 64 : (e + 1) * 64, :]


def prep_b(b, mask):
    return pl.pallas_call(
        prep_b_kernel,
        out_shape=jax.ShapeDtypeStruct((16, 64, 256), BF),
        in_specs=[FAR] * 2,
        out_specs=WHOLE,
        scratch_shapes=[pltpu.SMEM((4, 4), jnp.int32), VMEM((512, 512), BF), pltpu.SemaphoreType.DMA((2,))],
        compiler_params=params(PREP),
        cost_estimate=cost(512 * 512, 2 * 512 * 512 * 2),
    )(mask, b)


def arrange_kernel(*refs):
    bs, outs, sems = refs[:5], refs[5:7], refs[7]
    y, _, core, x = position()
    bands = (slice(0, 4), slice(0, 4), slice(0, 4), slice(0, 2), slice(2, 4))
    pairs = []
    for s, back in enumerate((0, 1, 3, 2, 2)):
        lanes = pl.ds(pl.multiple_of(lax.rem(y - back + 4, 4) * 256, 256), 256)
        for ahead in range(4):
            layer = lax.rem(x + ahead, 4)
            for half in range(2):
                side = core if half == 0 else 1 - core
                pairs.append((bs[s].at[:, layer, side], outs[half].at[ahead, bands[s], :, lanes]))
    fetch(pairs, sems)


def arrange(bs):
    return pl.pallas_call(
        arrange_kernel,
        out_shape=[jax.ShapeDtypeStruct((4, 4, 32, 1024), BF)] * 2,
        in_specs=[ANYWHERE] * 5,
        out_specs=[WHOLE] * 2,
        scratch_shapes=[pltpu.SemaphoreType.DMA((40,))],
        compiler_params=params(),
        cost_estimate=cost(0, 4 * 1024 * 1024),
    )(*bs)


def load(q, pieces, a_full, sems, tails, more=()):
    z = position()[1]
    pairs = list(more)
    for s in range(8):
        lanes = pl.ds(pl.multiple_of(lax.rem(z - s + 8, 8) * 128, 128), 128)
        pairs.append((pieces[s].at[0:MQ], a_full.at[:, lanes]))
    if q == 0:
        for s in range(8):
            pairs.append((pieces[s].at[MQ : MQ + TAIL], tails.at[s]))
    fetch(pairs, sems)


def multiply(a_full, b, rows):
    return lax.dot_general(
        a_full[rows, :],
        b[...].reshape(512, 1024),
        (((1,), (1,)), ((), ())),
        preferred_element_type=F32,
    )


def mask_rows(tails):
    _, z, core, x = position()
    row = lax.broadcasted_iota(jnp.int32, (TAIL, 128), 0)
    lane = lax.broadcasted_iota(jnp.int32, (TAIL, 128), 1)
    mask = jnp.zeros((TAIL, 128), F32)
    for s in range(8):
        band = 2 * lax.rem(z - s + 8, 8) + core
        values = tails[s].astype(F32)
        chosen = jnp.sum(jnp.where(row == z // 2, values, 0.0), axis=0, keepdims=True)
        column = jnp.sum(jnp.where(row == lane, chosen, 0.0), axis=1, keepdims=True)
        mask = jnp.where(lane // 32 * 4 + x == band, column, mask)
    return mask


def send_kernel(q, *refs):
    pieces, b, out = refs[:8], refs[8], refs[9]
    a_full, tails, sems = refs[10:]
    load(q, pieces, a_full, sems, tails)
    for part in range(4):
        rows = slice(part * (MQ // 4), (part + 1) * (MQ // 4))
        out[rows, :] = multiply(a_full, b, rows).astype(BF)
    if q == 0:
        out[MQ : MQ + TAIL, :] = jnp.zeros((TAIL, 512), BF)
        out[MQ : MQ + TAIL, 0:128] = mask_rows(tails).astype(BF)


def scratches():
    return [VMEM((MQ, 1024), BF), VMEM((8, TAIL, 128), BF), pltpu.SemaphoreType.DMA((17,))]


def send_half(q, pieces, b):
    return pl.pallas_call(
        lambda *refs: send_kernel(q, *refs),
        out_shape=jax.ShapeDtypeStruct((rows_of(q), 512), BF),
        in_specs=[ANYWHERE] * 8 + [WHOLE],
        out_specs=WHOLE,
        scratch_shapes=scratches(),
        compiler_params=params(),
        cost_estimate=cost(2 * MQ * 1024 * 512, MQ * 1024 * 2 + 1024 * 1024),
    )(*pieces, b)


def keep_kernel(q, *refs):
    pieces, b, received = refs[:8], refs[8], refs[9]
    own, outs = refs[10], refs[11:14]
    rest = refs[14:]
    if q == 0:
        mask, rest = rest[0], rest[1:]
    a_full, tails, sems, other = rest
    load(q, pieces, a_full, sems, tails, [(received, other)])
    for part in range(4):
        rows = slice(part * (MQ // 4), (part + 1) * (MQ // 4))
        value = multiply(a_full, b, rows) + other[rows, :].astype(F32)
        own[rows, :] = value[:, 0:128]
        for s in range(1, 4):
            outs[s - 1][rows, :] = value[:, s * 128 : (s + 1) * 128].astype(BF)
    if q == 0:
        mask[...] = mask_rows(tails) + other[MQ : MQ + TAIL, 0:128].astype(F32)


def keep_half(q, pieces, b, received):
    part = (MQ, 128)
    shapes = [jax.ShapeDtypeStruct(part, F32)] + [jax.ShapeDtypeStruct(part, BF)] * 3
    if q == 0:
        shapes.append(jax.ShapeDtypeStruct((TAIL, 128), F32))
    return pl.pallas_call(
        lambda *refs: keep_kernel(q, *refs),
        out_shape=shapes,
        in_specs=[ANYWHERE] * 8 + [WHOLE, ANYWHERE],
        out_specs=[WHOLE] * len(shapes),
        scratch_shapes=scratches() + [VMEM((rows_of(q), 512), BF)],
        compiler_params=params(),
        cost_estimate=cost(2 * MQ * 1024 * 512, MQ * 1024 * 2 + 2 * 1024 * 1024),
    )(*pieces, b, received)


def sum_kernel(*refs):
    mask, parts, out, flips, turned = refs[0], refs[1:-6], refs[-6], refs[-5:-1], refs[-1]
    y = position()[0]
    size = MQ // 4
    for xb in range(4):
        for q in range(NQ):
            own, first, second, third = parts[4 * q : 4 * q + 4]
            for j in range(4 // NQ):
                at = xb * size + j * 128
                rows = slice(at, at + 128)
                value = own[rows, :] + first[rows, :].astype(F32)
                value = value + second[rows, :].astype(F32) + third[rows, :].astype(F32)
                block = q * (4 // NQ) + j
                value = value * mask[xb * 4 + block : xb * 4 + block + 1, :]
                out[4 * block : 4 * block + 4, xb] = value.astype(BF).reshape(4, 32, 128)
                lanes = slice((xb * 4 + block) * 128, (xb * 4 + block + 1) * 128)
                turned[:, :, lanes] = value.T.astype(BF).reshape(4, 32, 128)
    for s in range(4):
        flips[s][...] = turned[lax.rem(y + s, 4)]


def sum_parts(mask, parts):
    return pl.pallas_call(
        sum_kernel,
        out_shape=[jax.ShapeDtypeStruct((16, 4, 32, 128), BF)] + [jax.ShapeDtypeStruct((32, 2048), BF)] * 4,
        in_specs=[WHOLE] * (1 + len(parts)),
        out_specs=[WHOLE] * 5,
        scratch_shapes=[VMEM((4, 32, 2048), BF)],
        compiler_params=params(),
        cost_estimate=cost(512 * 512 * 5, 512 * 512 * 14),
    )(mask, *parts)


def final_kernel(own, *refs):
    mirrored, out, ordered = refs[:4], refs[4], refs[5]
    y = position()[0]
    for s in range(4):
        ordered[lax.rem(y - s + 4, 4)] = mirrored[s][...]
    group = lax.broadcasted_iota(jnp.int32, (32, 128), 1) // 32
    for k_high in range(4):
        for layer in range(4):
            sources = [own[(4 * k_high + k) * 4 + layer].astype(F32) for k in range(4)]
            at = layer * 512 + k_high * 128
            for row in range(4):
                value = None
                for k in range(4):
                    shift = ((k - row) % 4) * 32
                    turned = pltpu.roll(sources[k], shift, 1) if shift else sources[k]
                    value = turned if value is None else jnp.where(group == k, turned, value)
                value = value + ordered[row, :, at : at + 128].astype(F32)
                out[:, row * 2048 + at : row * 2048 + at + 128] = value.astype(BF)


def finish(own, mirrored):
    return pl.pallas_call(
        final_kernel,
        out_shape=jax.ShapeDtypeStruct((32, 8192), BF),
        in_specs=[WHOLE] * 5,
        out_specs=WHOLE,
        scratch_shapes=[VMEM((4, 32, 2048), BF)],
        compiler_params=params(),
        cost_estimate=cost(32 * 8192 * 8, 3 * 32 * 8192 * 2),
    )(own, *mirrored)


def turn_z(value, shift):
    pairs = [(2 * z + c, 2 * ((z + shift) % 8) + c) for z in range(8) for c in range(2)]
    return lax.ppermute(value, "col", pairs)


def turn(value, axis, shift):
    return lax.ppermute(value, axis, [(i, (i + shift) % 4) for i in range(4)])


def per_device(density, response, density_mask, response_mask, result_mask):
    chunks = prep_a(density.reshape(2048, 128), density_mask.reshape(1, 16), result_mask.T)
    chunks, response = lax.optimization_barrier((chunks, response))
    b_send = prep_b(response.reshape(512, 512), response_mask.reshape(4, 4))

    b_own = lax.all_to_all(b_send, "col", 0, 0)

    gathered = [{0: chunk} for chunk in chunks]
    for step in range(1, 5):
        if step == 2:
            gathered[1][1], gathered[1][7], b_own = lax.optimization_barrier((gathered[1][1], gathered[1][7], b_own))
        for q in range(NQ):
            got = gathered[q]
            if step < 4 or q % 2 == 0:
                got[step] = turn_z(got[step - 1], 1)
            if step < 4 or q % 2 == 1:
                got[8 - step] = turn_z(got[(9 - step) % 8], -1)

    behind, ahead = turn(b_own, "row", 1), turn(b_own, "row", -1)
    bs = [b_own, behind, ahead, turn(behind[:8], "row", 1), turn(ahead[8:], "row", -1)]
    bs = [value.reshape(-1, 4, 2, 32, 256) for value in bs]

    kept_b, sent_b = arrange(bs)

    parts = []
    mask = None
    for q in range(NQ):
        pieces = [gathered[q][s] for s in range(8)]
        other = send_half(q, pieces, sent_b)
        received = lax.ppermute(other, "col", [(i, i ^ 1) for i in range(16)])
        kept = keep_half(q, pieces, kept_b, received)
        if q == 0:
            mask = kept[4]
        parts += [kept[0]] + [turn(kept[s], "layer", s) for s in (1, 2, 3)]

    product, *flips = sum_parts(mask, parts)
    own = lax.all_to_all(product.reshape(64, 32, 128), ("col", "layer"), 0, 0)
    mirrored = [flips[0]] + [turn(flips[s], "row", s) for s in (1, 2, 3)]
    return finish(own, mirrored).reshape(1, 1, 32, 8192)


def solution(mesh):
    placed = (
        P("row", "layer", "col"),
        P("layer", "row", "col"),
        P("row", "layer", "col"),
        P("layer", "row", "col"),
        P("row", "col"),
    )
    return jax.shard_map(
        per_device,
        mesh=mesh,
        in_specs=placed,
        out_specs=P(("row", "layer"), "col", None, None),
        check_vma=False,
    )
```

```python
import jax
import jax.numpy as jnp
from jax import lax
from jax.experimental import pallas as pl
from jax.experimental.pallas import tpu as pltpu
from jax.sharding import PartitionSpec as P

NQ = 2
MQ = 2048 // NQ
TAIL = 16
BF = jnp.bfloat16
F32 = jnp.float32
VMEM = pltpu.VMEM
WHOLE = pl.BlockSpec(memory_space=pltpu.VMEM)
FAR = pl.BlockSpec(memory_space=pltpu.HBM)
PREP = 60
ANYWHERE = pl.BlockSpec(memory_space=pl.ANY)


def params(mib=16):
    return pltpu.CompilerParams(vmem_limit_bytes=mib * 1024 * 1024)


def cost(flops, moved):
    return pl.CostEstimate(flops=flops, bytes_accessed=moved, transcendentals=0)


def position():
    place = lax.axis_index("col")
    return lax.axis_index("row"), place // 2, place % 2, lax.axis_index("layer")


def rows_of(q):
    return MQ + TAIL if q == 0 else MQ


def fetch(pairs, sems):
    copies = [pltpu.make_async_copy(source, to, sems.at[n]) for n, (source, to) in enumerate(pairs)]
    for copy in copies:
        copy.start()
    for copy in copies:
        copy.wait()


def prep_a_kernel(dm_in, a_in, rm_in, *rest):
    outs, (spare, dm, a, rm, sems) = rest[:NQ], rest[NQ:]
    fetch(((dm_in, dm), (a_in, a), (rm_in, rm)), sems)
    per = 4 // NQ
    for q in range(NQ):
        for xb in range(4):
            for j in range(per):
                block = xb * 4 + q * per + j
                keep = dm[0, block].astype(F32)
                value = a[block * 128 : (block + 1) * 128, :].astype(F32) * keep
                at = (xb * per + j) * 128
                outs[q][at : at + 128, :] = value.astype(BF)
    spare[...] = jnp.zeros_like(spare)
    spare[0:4, 0:16] = rm[...].astype(F32)
    outs[0][MQ : MQ + TAIL, :] = spare[...].astype(BF)


def prep_a(a, dm, rm):
    return pl.pallas_call(
        prep_a_kernel,
        out_shape=[jax.ShapeDtypeStruct((rows_of(q), 128), BF) for q in range(NQ)],
        in_specs=[FAR] * 3,
        out_specs=[WHOLE] * NQ,
        scratch_shapes=[
            VMEM((TAIL, 128), F32),
            pltpu.SMEM((1, 16), jnp.int32),
            VMEM((2048, 128), BF),
            VMEM((4, 16), jnp.int32),
            pltpu.SemaphoreType.DMA((3,)),
        ],
        compiler_params=params(PREP),
        cost_estimate=cost(2048 * 128, 2 * 2048 * 128 * 2),
    )(dm, a, rm)


def prep_b_kernel(mask_in, b_in, out, mask, b, sems):
    fetch(((mask_in, mask), (b_in, b)), sems)
    for tb in range(4):
        for cb in range(4):
            keep = mask[tb, cb].astype(F32)
            block = b[tb * 128 : (tb + 1) * 128, cb * 128 : (cb + 1) * 128].astype(F32) * keep
            flipped = block.T.astype(BF)
            lanes = slice((tb // 2) * 128, (tb // 2 + 1) * 128)
            for e in range(2):
                out[(2 * cb + e) * 2 + tb % 2, :, lanes] = flipped[e * 64 : (e + 1) * 64, :]


def prep_b(b, mask):
    return pl.pallas_call(
        prep_b_kernel,
        out_shape=jax.ShapeDtypeStruct((16, 64, 256), BF),
        in_specs=[FAR] * 2,
        out_specs=WHOLE,
        scratch_shapes=[pltpu.SMEM((4, 4), jnp.int32), VMEM((512, 512), BF), pltpu.SemaphoreType.DMA((2,))],
        compiler_params=params(PREP),
        cost_estimate=cost(512 * 512, 2 * 512 * 512 * 2),
    )(mask, b)


def arrange_kernel(*refs):
    bs, outs, sems = refs[:5], refs[5:7], refs[7]
    y, _, core, x = position()
    bands = (slice(0, 4), slice(0, 4), slice(0, 4), slice(0, 2), slice(2, 4))
    pairs = []
    for s, back in enumerate((0, 1, 3, 2, 2)):
        lanes = pl.ds(pl.multiple_of(lax.rem(y - back + 4, 4) * 256, 256), 256)
        for ahead in range(4):
            layer = lax.rem(x + ahead, 4)
            for half in range(2):
                side = core if half == 0 else 1 - core
                pairs.append((bs[s].at[:, layer, side], outs[half].at[ahead, bands[s], :, lanes]))
    fetch(pairs, sems)


def arrange(bs):
    return pl.pallas_call(
        arrange_kernel,
        out_shape=[jax.ShapeDtypeStruct((4, 4, 32, 1024), BF)] * 2,
        in_specs=[ANYWHERE] * 5,
        out_specs=[WHOLE] * 2,
        scratch_shapes=[pltpu.SemaphoreType.DMA((40,))],
        compiler_params=params(),
        cost_estimate=cost(0, 4 * 1024 * 1024),
    )(*bs)


def load(q, pieces, a_full, sems, tails, more=()):
    z = position()[1]
    pairs = list(more)
    for s in range(8):
        lanes = pl.ds(pl.multiple_of(lax.rem(z - s + 8, 8) * 128, 128), 128)
        pairs.append((pieces[s].at[0:MQ], a_full.at[:, lanes]))
    if q == 0:
        for s in range(8):
            pairs.append((pieces[s].at[MQ : MQ + TAIL], tails.at[s]))
    fetch(pairs, sems)


def multiply(a_full, b, rows):
    return lax.dot_general(
        a_full[rows, :],
        b[...].reshape(512, 1024),
        (((1,), (1,)), ((), ())),
        preferred_element_type=F32,
    )


def mask_rows(tails):
    _, z, core, x = position()
    row = lax.broadcasted_iota(jnp.int32, (TAIL, 128), 0)
    lane = lax.broadcasted_iota(jnp.int32, (TAIL, 128), 1)
    mask = jnp.zeros((TAIL, 128), F32)
    for s in range(8):
        band = 2 * lax.rem(z - s + 8, 8) + core
        values = tails[s].astype(F32)
        chosen = jnp.sum(jnp.where(row == z // 2, values, 0.0), axis=0, keepdims=True)
        column = jnp.sum(jnp.where(row == lane, chosen, 0.0), axis=1, keepdims=True)
        mask = jnp.where(lane // 32 * 4 + x == band, column, mask)
    return mask


def send_kernel(q, *refs):
    pieces, b, out = refs[:8], refs[8], refs[9]
    a_full, tails, sems = refs[10:]
    load(q, pieces, a_full, sems, tails)
    for part in range(4):
        rows = slice(part * (MQ // 4), (part + 1) * (MQ // 4))
        out[rows, :] = multiply(a_full, b, rows).astype(BF)
    if q == 0:
        out[MQ : MQ + TAIL, :] = jnp.zeros((TAIL, 512), BF)
        out[MQ : MQ + TAIL, 0:128] = mask_rows(tails).astype(BF)


def scratches():
    return [VMEM((MQ, 1024), BF), VMEM((8, TAIL, 128), BF), pltpu.SemaphoreType.DMA((17,))]


def send_half(q, pieces, b):
    return pl.pallas_call(
        lambda *refs: send_kernel(q, *refs),
        out_shape=jax.ShapeDtypeStruct((rows_of(q), 512), BF),
        in_specs=[ANYWHERE] * 8 + [WHOLE],
        out_specs=WHOLE,
        scratch_shapes=scratches(),
        compiler_params=params(),
        cost_estimate=cost(2 * MQ * 1024 * 512, MQ * 1024 * 2 + 1024 * 1024),
    )(*pieces, b)


def keep_kernel(q, *refs):
    pieces, b, received = refs[:8], refs[8], refs[9]
    own, behind, ahead, upper, lower = refs[10:15]
    rest = refs[15:]
    if q == 0:
        mask, rest = rest[0], rest[1:]
    a_full, tails, sems, other = rest
    load(q, pieces, a_full, sems, tails, [(received, other)])
    for part in range(4):
        rows = slice(part * (MQ // 4), (part + 1) * (MQ // 4))
        value = multiply(a_full, b, rows) + other[rows, :].astype(F32)
        own[rows, :] = value[:, 0:128]
        ahead[rows, :] = value[:, 128:256]
        behind[rows, :] = value[:, 384:512]
        half = upper if part < 2 else lower
        at = (part % 2) * (MQ // 4)
        half[at : at + MQ // 4, :] = value[:, 256:384].astype(BF)
    if q == 0:
        mask[...] = mask_rows(tails) + other[MQ : MQ + TAIL, 0:128].astype(F32)


def keep_half(q, pieces, b, received):
    shapes = [jax.ShapeDtypeStruct((MQ, 128), F32)] * 3 + [jax.ShapeDtypeStruct((MQ // 2, 128), BF)] * 2
    if q == 0:
        shapes.append(jax.ShapeDtypeStruct((TAIL, 128), F32))
    return pl.pallas_call(
        lambda *refs: keep_kernel(q, *refs),
        out_shape=shapes,
        in_specs=[ANYWHERE] * 8 + [WHOLE, ANYWHERE],
        out_specs=[WHOLE] * len(shapes),
        scratch_shapes=scratches() + [VMEM((rows_of(q), 512), BF)],
        compiler_params=params(),
        cost_estimate=cost(2 * MQ * 1024 * 512, MQ * 1024 * 2 + 2 * 1024 * 1024),
    )(*pieces, b, received)


def relay_kernel(behind, ahead, upper, lower, behind_out, ahead_out):
    half = MQ // 2
    ahead_out[0:half, :] = (ahead[0:half, :] + upper[...].astype(F32)).astype(BF)
    ahead_out[half:MQ, :] = ahead[half:MQ, :].astype(BF)
    behind_out[0:half, :] = behind[0:half, :].astype(BF)
    behind_out[half:MQ, :] = (behind[half:MQ, :] + lower[...].astype(F32)).astype(BF)


def relay(behind, ahead, upper, lower):
    return pl.pallas_call(
        relay_kernel,
        out_shape=[jax.ShapeDtypeStruct((MQ, 128), BF)] * 2,
        in_specs=[WHOLE] * 4,
        out_specs=[WHOLE] * 2,
        compiler_params=params(),
        cost_estimate=cost(MQ * 128 * 2, MQ * 128 * 14),
    )(behind, ahead, upper, lower)


def sum_kernel(*refs):
    mask, parts, out, flips, turned = refs[0], refs[1:-6], refs[-6], refs[-5:-1], refs[-1]
    y = position()[0]
    size = MQ // 4
    for xb in range(4):
        for q in range(NQ):
            own, first, second = parts[3 * q : 3 * q + 3]
            for j in range(4 // NQ):
                at = xb * size + j * 128
                rows = slice(at, at + 128)
                value = own[rows, :] + first[rows, :].astype(F32) + second[rows, :].astype(F32)
                block = q * (4 // NQ) + j
                value = value * mask[xb * 4 + block : xb * 4 + block + 1, :]
                out[4 * block : 4 * block + 4, xb] = value.astype(BF).reshape(4, 32, 128)
                lanes = slice((xb * 4 + block) * 128, (xb * 4 + block + 1) * 128)
                turned[:, :, lanes] = value.T.astype(BF).reshape(4, 32, 128)
    for s in range(4):
        flips[s][...] = turned[lax.rem(y + s, 4)]


def sum_parts(mask, parts):
    return pl.pallas_call(
        sum_kernel,
        out_shape=[jax.ShapeDtypeStruct((16, 4, 32, 128), BF)] + [jax.ShapeDtypeStruct((32, 2048), BF)] * 4,
        in_specs=[WHOLE] * (1 + len(parts)),
        out_specs=[WHOLE] * 5,
        scratch_shapes=[VMEM((4, 32, 2048), BF)],
        compiler_params=params(),
        cost_estimate=cost(512 * 512 * 5, 512 * 512 * 14),
    )(mask, *parts)


def final_kernel(own, *refs):
    mirrored, out, ordered = refs[:4], refs[4], refs[5]
    y = position()[0]
    for s in range(4):
        ordered[lax.rem(y - s + 4, 4)] = mirrored[s][...]
    group = lax.broadcasted_iota(jnp.int32, (32, 128), 1) // 32
    for k_high in range(4):
        for layer in range(4):
            sources = [own[(4 * k_high + k) * 4 + layer].astype(F32) for k in range(4)]
            at = layer * 512 + k_high * 128
            for row in range(4):
                value = None
                for k in range(4):
                    shift = ((k - row) % 4) * 32
                    turned = pltpu.roll(sources[k], shift, 1) if shift else sources[k]
                    value = turned if value is None else jnp.where(group == k, turned, value)
                value = value + ordered[row, :, at : at + 128].astype(F32)
                out[:, row * 2048 + at : row * 2048 + at + 128] = value.astype(BF)


def finish(own, mirrored):
    return pl.pallas_call(
        final_kernel,
        out_shape=jax.ShapeDtypeStruct((32, 8192), BF),
        in_specs=[WHOLE] * 5,
        out_specs=WHOLE,
        scratch_shapes=[VMEM((4, 32, 2048), BF)],
        compiler_params=params(),
        cost_estimate=cost(32 * 8192 * 8, 3 * 32 * 8192 * 2),
    )(own, *mirrored)


def turn_z(value, shift):
    pairs = [(2 * z + c, 2 * ((z + shift) % 8) + c) for z in range(8) for c in range(2)]
    return lax.ppermute(value, "col", pairs)


def turn(value, axis, shift):
    return lax.ppermute(value, axis, [(i, (i + shift) % 4) for i in range(4)])


def per_device(density, response, density_mask, response_mask, result_mask):
    chunks = prep_a(density.reshape(2048, 128), density_mask.reshape(1, 16), result_mask.T)
    chunks, response = lax.optimization_barrier((chunks, response))
    b_send = prep_b(response.reshape(512, 512), response_mask.reshape(4, 4))

    b_own = lax.all_to_all(b_send, "col", 0, 0)

    gathered = [{0: chunk} for chunk in chunks]
    for step in range(1, 5):
        if step == 2:
            gathered[1][1], gathered[1][7], b_own = lax.optimization_barrier((gathered[1][1], gathered[1][7], b_own))
        for q in range(NQ):
            got = gathered[q]
            if step < 4 or q % 2 == 0:
                got[step] = turn_z(got[step - 1], 1)
            if step < 4 or q % 2 == 1:
                got[8 - step] = turn_z(got[(9 - step) % 8], -1)

    behind, ahead = turn(b_own, "row", 1), turn(b_own, "row", -1)
    bs = [b_own, behind, ahead, turn(behind[:8], "row", 1), turn(ahead[8:], "row", -1)]
    bs = [value.reshape(-1, 4, 2, 32, 256) for value in bs]

    kept_b, sent_b = arrange(bs)

    parts = []
    mask = None
    for q in range(NQ):
        pieces = [gathered[q][s] for s in range(8)]
        other = send_half(q, pieces, sent_b)
        received = lax.ppermute(other, "col", [(i, i ^ 1) for i in range(16)])
        kept = keep_half(q, pieces, kept_b, received)
        if q == 0:
            mask = kept[5]
        own_part, back, front, upper, lower = kept[:5]
        back, front = relay(back, front, turn(upper, "layer", 1), turn(lower, "layer", -1))
        parts += [own_part, turn(front, "layer", 1), turn(back, "layer", -1)]

    product, *flips = sum_parts(mask, parts)
    own = lax.all_to_all(product.reshape(64, 32, 128), ("col", "layer"), 0, 0)
    mirrored = [flips[0]] + [turn(flips[s], "row", s) for s in (1, 2, 3)]
    return finish(own, mirrored).reshape(1, 1, 32, 8192)


def solution(mesh):
    placed = (
        P("row", "layer", "col"),
        P("layer", "row", "col"),
        P("row", "layer", "col"),
        P("layer", "row", "col"),
        P("row", "col"),
    )
    return jax.shard_map(
        per_device,
        mesh=mesh,
        in_specs=placed,
        out_specs=P(("row", "layer"), "col", None, None),
        check_vma=False,
    )
```

```python
import jax
import jax.numpy as jnp
from jax import lax
from jax.experimental import pallas as pl
from jax.experimental.pallas import tpu as pltpu
from jax.sharding import PartitionSpec as P

NQ = 2
MQ = 2048 // NQ
TAIL = 16
BF = jnp.bfloat16
F32 = jnp.float32
VMEM = pltpu.VMEM
WHOLE = pl.BlockSpec(memory_space=pltpu.VMEM)
FAR = pl.BlockSpec(memory_space=pltpu.HBM)
PREP = 60
ANYWHERE = pl.BlockSpec(memory_space=pl.ANY)


def params(mib=16):
    return pltpu.CompilerParams(vmem_limit_bytes=mib * 1024 * 1024)


def cost(flops, moved):
    return pl.CostEstimate(flops=flops, bytes_accessed=moved, transcendentals=0)


def position():
    place = lax.axis_index("col")
    return lax.axis_index("row"), place // 2, place % 2, lax.axis_index("layer")


def rows_of(q):
    return MQ + TAIL if q == 0 else MQ


def fetch(pairs, sems):
    copies = [pltpu.make_async_copy(source, to, sems.at[n]) for n, (source, to) in enumerate(pairs)]
    for copy in copies:
        copy.start()
    for copy in copies:
        copy.wait()


def prep_a_kernel(dm_in, a_in, rm_in, *rest):
    outs, (spare, dm, a, rm, sems) = rest[:NQ], rest[NQ:]
    fetch(((dm_in, dm), (a_in, a), (rm_in, rm)), sems)
    per = 4 // NQ
    for q in range(NQ):
        for xb in range(4):
            for j in range(per):
                block = xb * 4 + q * per + j
                keep = dm[0, block].astype(F32)
                value = a[block * 128 : (block + 1) * 128, :].astype(F32) * keep
                at = (xb * per + j) * 128
                outs[q][at : at + 128, :] = value.astype(BF)
    spare[...] = jnp.zeros_like(spare)
    spare[0:4, 0:16] = rm[...].astype(F32)
    outs[0][MQ : MQ + TAIL, :] = spare[...].astype(BF)


def prep_a(a, dm, rm):
    return pl.pallas_call(
        prep_a_kernel,
        out_shape=[jax.ShapeDtypeStruct((rows_of(q), 128), BF) for q in range(NQ)],
        in_specs=[FAR] * 3,
        out_specs=[WHOLE] * NQ,
        scratch_shapes=[
            VMEM((TAIL, 128), F32),
            pltpu.SMEM((1, 16), jnp.int32),
            VMEM((2048, 128), BF),
            VMEM((4, 16), jnp.int32),
            pltpu.SemaphoreType.DMA((3,)),
        ],
        compiler_params=params(PREP),
        cost_estimate=cost(2048 * 128, 2 * 2048 * 128 * 2),
    )(dm, a, rm)


def prep_b_kernel(mask_in, b_in, out, mask, b, sems):
    fetch(((mask_in, mask), (b_in, b)), sems)
    for tb in range(4):
        for cb in range(4):
            keep = mask[tb, cb].astype(F32)
            block = b[tb * 128 : (tb + 1) * 128, cb * 128 : (cb + 1) * 128].astype(F32) * keep
            flipped = block.T.astype(BF)
            lanes = slice((tb // 2) * 128, (tb // 2 + 1) * 128)
            for e in range(2):
                out[(2 * cb + e) * 2 + tb % 2, :, lanes] = flipped[e * 64 : (e + 1) * 64, :]


def prep_b(b, mask):
    return pl.pallas_call(
        prep_b_kernel,
        out_shape=jax.ShapeDtypeStruct((16, 64, 256), BF),
        in_specs=[FAR] * 2,
        out_specs=WHOLE,
        scratch_shapes=[pltpu.SMEM((4, 4), jnp.int32), VMEM((512, 512), BF), pltpu.SemaphoreType.DMA((2,))],
        compiler_params=params(PREP),
        cost_estimate=cost(512 * 512, 2 * 512 * 512 * 2),
    )(mask, b)


def arrange_kernel(*refs):
    bs, outs, sems = refs[:5], refs[5:7], refs[7]
    y, _, core, x = position()
    bands = (slice(0, 4), slice(0, 4), slice(0, 4), slice(0, 2), slice(2, 4))
    pairs = []
    for s, back in enumerate((0, 1, 3, 2, 2)):
        lanes = pl.ds(pl.multiple_of(lax.rem(y - back + 4, 4) * 256, 256), 256)
        for ahead in range(4):
            layer = lax.rem(x + ahead, 4)
            for half in range(2):
                side = core if half == 0 else 1 - core
                pairs.append((bs[s].at[:, layer, side], outs[half].at[ahead, bands[s], :, lanes]))
    fetch(pairs, sems)


def arrange(bs):
    return pl.pallas_call(
        arrange_kernel,
        out_shape=[jax.ShapeDtypeStruct((4, 4, 32, 1024), BF)] * 2,
        in_specs=[ANYWHERE] * 5,
        out_specs=[WHOLE] * 2,
        scratch_shapes=[pltpu.SemaphoreType.DMA((40,))],
        compiler_params=params(),
        cost_estimate=cost(0, 4 * 1024 * 1024),
    )(*bs)


def load(q, pieces, a_full, sems, tails, more=()):
    z = position()[1]
    pairs = list(more)
    for s in range(8):
        lanes = pl.ds(pl.multiple_of(lax.rem(z - s + 8, 8) * 128, 128), 128)
        pairs.append((pieces[s].at[0:MQ], a_full.at[:, lanes]))
    if q == 0:
        for s in range(8):
            pairs.append((pieces[s].at[MQ : MQ + TAIL], tails.at[s]))
    fetch(pairs, sems)


def multiply(a_full, b, rows):
    return lax.dot_general(
        a_full[rows, :],
        b[...].reshape(512, 1024),
        (((1,), (1,)), ((), ())),
        preferred_element_type=F32,
    )


def mask_rows(tails):
    _, z, core, x = position()
    row = lax.broadcasted_iota(jnp.int32, (TAIL, 128), 0)
    lane = lax.broadcasted_iota(jnp.int32, (TAIL, 128), 1)
    mask = jnp.zeros((TAIL, 128), F32)
    for s in range(8):
        band = 2 * lax.rem(z - s + 8, 8) + core
        values = tails[s].astype(F32)
        chosen = jnp.sum(jnp.where(row == z // 2, values, 0.0), axis=0, keepdims=True)
        column = jnp.sum(jnp.where(row == lane, chosen, 0.0), axis=1, keepdims=True)
        mask = jnp.where(lane // 32 * 4 + x == band, column, mask)
    return mask


def send_kernel(q, *refs):
    pieces, b, out = refs[:8], refs[8], refs[9]
    a_full, tails, sems = refs[10:]
    load(q, pieces, a_full, sems, tails)
    for part in range(4):
        rows = slice(part * (MQ // 4), (part + 1) * (MQ // 4))
        out[rows, :] = multiply(a_full, b, rows).astype(BF)
    if q == 0:
        out[MQ : MQ + TAIL, :] = jnp.zeros((TAIL, 512), BF)
        out[MQ : MQ + TAIL, 0:128] = mask_rows(tails).astype(BF)


def scratches():
    return [VMEM((MQ, 1024), BF), VMEM((8, TAIL, 128), BF), pltpu.SemaphoreType.DMA((17,))]


def send_half(q, pieces, b):
    return pl.pallas_call(
        lambda *refs: send_kernel(q, *refs),
        out_shape=jax.ShapeDtypeStruct((rows_of(q), 512), BF),
        in_specs=[ANYWHERE] * 8 + [WHOLE],
        out_specs=WHOLE,
        scratch_shapes=scratches(),
        compiler_params=params(),
        cost_estimate=cost(2 * MQ * 1024 * 512, MQ * 1024 * 2 + 1024 * 1024),
    )(*pieces, b)


def keep_kernel(q, *refs):
    pieces, b, received = refs[:8], refs[8], refs[9]
    own, behind, ahead, upper, lower = refs[10:15]
    rest = refs[15:]
    if q == 0:
        mask, rest = rest[0], rest[1:]
    a_full, tails, sems, other = rest
    load(q, pieces, a_full, sems, tails, [(received, other)])
    for part in range(4):
        rows = slice(part * (MQ // 4), (part + 1) * (MQ // 4))
        value = multiply(a_full, b, rows) + other[rows, :].astype(F32)
        own[rows, :] = value[:, 0:128]
        ahead[rows, :] = value[:, 128:256]
        behind[rows, :] = value[:, 384:512]
        half = upper if part < 2 else lower
        at = (part % 2) * (MQ // 4)
        half[at : at + MQ // 4, :] = value[:, 256:384].astype(BF)
    if q == 0:
        mask[...] = mask_rows(tails) + other[MQ : MQ + TAIL, 0:128].astype(F32)


def keep_half(q, pieces, b, received):
    shapes = [jax.ShapeDtypeStruct((MQ, 128), F32)] * 3 + [jax.ShapeDtypeStruct((MQ // 2, 128), BF)] * 2
    if q == 0:
        shapes.append(jax.ShapeDtypeStruct((TAIL, 128), F32))
    return pl.pallas_call(
        lambda *refs: keep_kernel(q, *refs),
        out_shape=shapes,
        in_specs=[ANYWHERE] * 8 + [WHOLE, ANYWHERE],
        out_specs=[WHOLE] * len(shapes),
        scratch_shapes=scratches() + [VMEM((rows_of(q), 512), BF)],
        compiler_params=params(),
        cost_estimate=cost(2 * MQ * 1024 * 512, MQ * 1024 * 2 + 2 * 1024 * 1024),
    )(*pieces, b, received)


def relay_kernel(behind, ahead, upper, lower, behind_out, ahead_out):
    half = MQ // 2
    ahead_out[0:half, :] = (ahead[0:half, :] + upper[...].astype(F32)).astype(BF)
    ahead_out[half:MQ, :] = ahead[half:MQ, :].astype(BF)
    behind_out[0:half, :] = behind[0:half, :].astype(BF)
    behind_out[half:MQ, :] = (behind[half:MQ, :] + lower[...].astype(F32)).astype(BF)


def relay(behind, ahead, upper, lower):
    return pl.pallas_call(
        relay_kernel,
        out_shape=[jax.ShapeDtypeStruct((MQ, 128), BF)] * 2,
        in_specs=[WHOLE] * 4,
        out_specs=[WHOLE] * 2,
        compiler_params=params(),
        cost_estimate=cost(MQ * 128 * 2, MQ * 128 * 14),
    )(behind, ahead, upper, lower)


def sum_kernel(*refs):
    mask, parts, out, flips, turned = refs[0], refs[1:-6], refs[-6], refs[-5:-1], refs[-1]
    y = position()[0]
    size = MQ // 4
    for xb in range(4):
        for q in range(NQ):
            own, first, second = parts[3 * q : 3 * q + 3]
            for j in range(4 // NQ):
                at = xb * size + j * 128
                rows = slice(at, at + 128)
                value = own[rows, :] + first[rows, :].astype(F32) + second[rows, :].astype(F32)
                block = q * (4 // NQ) + j
                value = value * mask[xb * 4 + block : xb * 4 + block + 1, :]
                out[4 * block : 4 * block + 4, xb] = value.astype(BF).reshape(4, 32, 128)
                lanes = slice((xb * 4 + block) * 128, (xb * 4 + block + 1) * 128)
                turned[:, :, lanes] = value.T.astype(BF).reshape(4, 32, 128)
    for s in range(4):
        flips[s][...] = turned[lax.rem(y + s, 4)]


def sum_parts(mask, parts):
    return pl.pallas_call(
        sum_kernel,
        out_shape=[jax.ShapeDtypeStruct((16, 4, 32, 128), BF)] + [jax.ShapeDtypeStruct((32, 2048), BF)] * 4,
        in_specs=[WHOLE] * (1 + len(parts)),
        out_specs=[WHOLE] * 5,
        scratch_shapes=[VMEM((4, 32, 2048), BF)],
        compiler_params=params(),
        cost_estimate=cost(512 * 512 * 5, 512 * 512 * 14),
    )(mask, *parts)


def final_kernel(own, *refs):
    mirrored, out, ordered = refs[:4], refs[4], refs[5]
    y = position()[0]
    for s in range(4):
        ordered[lax.rem(y - s + 4, 4)] = mirrored[s][...]
    group = lax.broadcasted_iota(jnp.int32, (32, 128), 1) // 32
    for k_high in range(4):
        for layer in range(4):
            sources = [own[(4 * k_high + k) * 4 + layer].astype(F32) for k in range(4)]
            at = layer * 512 + k_high * 128
            for row in range(4):
                value = None
                for k in range(4):
                    shift = ((k - row) % 4) * 32
                    turned = pltpu.roll(sources[k], shift, 1) if shift else sources[k]
                    value = turned if value is None else jnp.where(group == k, turned, value)
                value = value + ordered[row, :, at : at + 128].astype(F32)
                out[:, row * 2048 + at : row * 2048 + at + 128] = value.astype(BF)


def finish(own, mirrored):
    return pl.pallas_call(
        final_kernel,
        out_shape=jax.ShapeDtypeStruct((32, 8192), BF),
        in_specs=[WHOLE] * 5,
        out_specs=WHOLE,
        scratch_shapes=[VMEM((4, 32, 2048), BF)],
        compiler_params=params(),
        cost_estimate=cost(32 * 8192 * 8, 3 * 32 * 8192 * 2),
    )(own, *mirrored)


def turn_z(value, shift):
    pairs = [(2 * z + c, 2 * ((z + shift) % 8) + c) for z in range(8) for c in range(2)]
    return lax.ppermute(value, "col", pairs)


def turn(value, axis, shift):
    return lax.ppermute(value, axis, [(i, (i + shift) % 4) for i in range(4)])


def per_device(density, response, density_mask, response_mask, result_mask):
    chunks = prep_a(density.reshape(2048, 128), density_mask.reshape(1, 16), result_mask.T)
    chunks, response = lax.optimization_barrier((chunks, response))
    b_send = prep_b(response.reshape(512, 512), response_mask.reshape(4, 4))

    b_own = lax.all_to_all(b_send, "col", 0, 0)
    gathered = [{0: chunk} for chunk in chunks]

    def ring(q, step):
        got = gathered[q]
        if step < 4 or q % 2 == 0:
            got[step] = turn_z(got[step - 1], 1)
        if step < 4 or q % 2 == 1:
            got[8 - step] = turn_z(got[(9 - step) % 8], -1)

    ring(0, 1)
    ring(1, 1)
    (gathered[1][1], gathered[1][7], b_own) = lax.optimization_barrier((gathered[1][1], gathered[1][7], b_own))
    behind, ahead = turn(b_own, "row", 1), turn(b_own, "row", -1)
    ring(0, 2)
    ring(1, 2)
    (gathered[1][2], gathered[1][6], behind, ahead) = lax.optimization_barrier((gathered[1][2], gathered[1][6], behind, ahead))
    bs = [b_own, behind, ahead, turn(behind[:8], "row", 1), turn(ahead[8:], "row", -1)]
    ring(0, 3)
    ring(1, 3)
    ring(0, 4)
    ring(1, 4)

    bs = [value.reshape(-1, 4, 2, 32, 256) for value in bs]

    kept_b, sent_b = arrange(bs)

    parts = []
    mask = None
    for q in range(NQ):
        pieces = [gathered[q][s] for s in range(8)]
        other = send_half(q, pieces, sent_b)
        received = lax.ppermute(other, "col", [(i, i ^ 1) for i in range(16)])
        kept = keep_half(q, pieces, kept_b, received)
        if q == 0:
            mask = kept[5]
        own_part, back, front, upper, lower = kept[:5]
        back, front = relay(back, front, turn(upper, "layer", 1), turn(lower, "layer", -1))
        parts += [own_part, turn(front, "layer", 1), turn(back, "layer", -1)]

    product, *flips = sum_parts(mask, parts)
    own = lax.all_to_all(product.reshape(64, 32, 128), ("col", "layer"), 0, 0)
    mirrored = [flips[0]] + [turn(flips[s], "row", s) for s in (1, 2, 3)]
    return finish(own, mirrored).reshape(1, 1, 32, 8192)


def solution(mesh):
    placed = (
        P("row", "layer", "col"),
        P("layer", "row", "col"),
        P("row", "layer", "col"),
        P("layer", "row", "col"),
        P("row", "col"),
    )
    return jax.shard_map(
        per_device,
        mesh=mesh,
        in_specs=placed,
        out_specs=P(("row", "layer"), "col", None, None),
        check_vma=False,
    )
```

```python
import jax
import jax.numpy as jnp
from jax import lax
from jax.experimental import pallas as pl
from jax.experimental.pallas import tpu as pltpu
from jax.sharding import PartitionSpec as P

NQ = 2
MQ = 2048 // NQ
TAIL = 16
BF = jnp.bfloat16
F32 = jnp.float32
VMEM = pltpu.VMEM
WHOLE = pl.BlockSpec(memory_space=pltpu.VMEM)
FAR = pl.BlockSpec(memory_space=pltpu.HBM)
PREP = 60
ANYWHERE = pl.BlockSpec(memory_space=pl.ANY)


def params(mib=16):
    return pltpu.CompilerParams(vmem_limit_bytes=mib * 1024 * 1024)


def cost(flops, moved):
    return pl.CostEstimate(flops=flops, bytes_accessed=moved, transcendentals=0)


def position():
    place = lax.axis_index("col")
    return lax.axis_index("row"), place // 2, place % 2, lax.axis_index("layer")


def rows_of(q):
    return MQ + TAIL if q == 0 else MQ


def fetch(pairs, sems):
    copies = [pltpu.make_async_copy(source, to, sems.at[n]) for n, (source, to) in enumerate(pairs)]
    for copy in copies:
        copy.start()
    for copy in copies:
        copy.wait()


def prep_a_kernel(dm_in, a_in, rm_in, *rest):
    outs, (spare, dm, a, rm, sems) = rest[:NQ], rest[NQ:]
    fetch(((dm_in, dm), (a_in, a), (rm_in, rm)), sems)
    per = 4 // NQ
    for q in range(NQ):
        for xb in range(4):
            for j in range(per):
                block = xb * 4 + q * per + j
                keep = dm[0, block].astype(F32)
                value = a[block * 128 : (block + 1) * 128, :].astype(F32) * keep
                at = (xb * per + j) * 128
                outs[q][at : at + 128, :] = value.astype(BF)
    spare[...] = jnp.zeros_like(spare)
    spare[0:4, 0:16] = rm[...].astype(F32)
    outs[0][MQ : MQ + TAIL, :] = spare[...].astype(BF)


def prep_a(a, dm, rm):
    return pl.pallas_call(
        prep_a_kernel,
        out_shape=[jax.ShapeDtypeStruct((rows_of(q), 128), BF) for q in range(NQ)],
        in_specs=[FAR] * 3,
        out_specs=[WHOLE] * NQ,
        scratch_shapes=[
            VMEM((TAIL, 128), F32),
            pltpu.SMEM((1, 16), jnp.int32),
            VMEM((2048, 128), BF),
            VMEM((4, 16), jnp.int32),
            pltpu.SemaphoreType.DMA((3,)),
        ],
        compiler_params=params(PREP),
        cost_estimate=cost(2048 * 128, 2 * 2048 * 128 * 2),
    )(dm, a, rm)


def prep_b_kernel(mask_in, b_in, out, mask, b, sems):
    fetch(((mask_in, mask), (b_in, b)), sems)
    for tb in range(4):
        for cb in range(4):
            keep = mask[tb, cb].astype(F32)
            block = b[tb * 128 : (tb + 1) * 128, cb * 128 : (cb + 1) * 128].astype(F32) * keep
            flipped = block.T.astype(BF)
            lanes = slice((tb // 2) * 128, (tb // 2 + 1) * 128)
            for e in range(2):
                out[(2 * cb + e) * 2 + tb % 2, :, lanes] = flipped[e * 64 : (e + 1) * 64, :]


def prep_b(b, mask):
    return pl.pallas_call(
        prep_b_kernel,
        out_shape=jax.ShapeDtypeStruct((16, 64, 256), BF),
        in_specs=[FAR] * 2,
        out_specs=WHOLE,
        scratch_shapes=[pltpu.SMEM((4, 4), jnp.int32), VMEM((512, 512), BF), pltpu.SemaphoreType.DMA((2,))],
        compiler_params=params(PREP),
        cost_estimate=cost(512 * 512, 2 * 512 * 512 * 2),
    )(mask, b)


def arrange_kernel(*refs):
    bs, outs, sems = refs[:5], refs[5:7], refs[7]
    y, _, core, x = position()
    bands = (slice(0, 4), slice(0, 4), slice(0, 4), slice(0, 2), slice(2, 4))
    pairs = []
    for s, back in enumerate((0, 1, 3, 2, 2)):
        lanes = pl.ds(pl.multiple_of(lax.rem(y - back + 4, 4) * 256, 256), 256)
        for ahead in range(4):
            layer = lax.rem(x + ahead, 4)
            for half in range(2):
                side = core if half == 0 else 1 - core
                pairs.append((bs[s].at[:, layer, side], outs[half].at[ahead, bands[s], :, lanes]))
    fetch(pairs, sems)


def arrange(bs):
    return pl.pallas_call(
        arrange_kernel,
        out_shape=[jax.ShapeDtypeStruct((4, 4, 32, 1024), BF)] * 2,
        in_specs=[ANYWHERE] * 5,
        out_specs=[WHOLE] * 2,
        scratch_shapes=[pltpu.SemaphoreType.DMA((40,))],
        compiler_params=params(),
        cost_estimate=cost(0, 4 * 1024 * 1024),
    )(*bs)


def load(q, pieces, a_full, sems, tails, more=()):
    z = position()[1]
    pairs = list(more)
    for s in range(8):
        lanes = pl.ds(pl.multiple_of(lax.rem(z - s + 8, 8) * 128, 128), 128)
        pairs.append((pieces[s].at[0:MQ], a_full.at[:, lanes]))
    if q == 0:
        for s in range(8):
            pairs.append((pieces[s].at[MQ : MQ + TAIL], tails.at[s]))
    fetch(pairs, sems)


def multiply(a_full, b, rows):
    return lax.dot_general(
        a_full[rows, :],
        b[...].reshape(512, 1024),
        (((1,), (1,)), ((), ())),
        preferred_element_type=F32,
    )


def mask_rows(tails):
    _, z, core, x = position()
    row = lax.broadcasted_iota(jnp.int32, (TAIL, 128), 0)
    lane = lax.broadcasted_iota(jnp.int32, (TAIL, 128), 1)
    mask = jnp.zeros((TAIL, 128), F32)
    for s in range(8):
        band = 2 * lax.rem(z - s + 8, 8) + core
        values = tails[s].astype(F32)
        chosen = jnp.sum(jnp.where(row == z // 2, values, 0.0), axis=0, keepdims=True)
        column = jnp.sum(jnp.where(row == lane, chosen, 0.0), axis=1, keepdims=True)
        mask = jnp.where(lane // 32 * 4 + x == band, column, mask)
    return mask


def send_kernel(q, *refs):
    pieces, b, out = refs[:8], refs[8], refs[9]
    a_full, tails, sems = refs[10:]
    load(q, pieces, a_full, sems, tails)
    for part in range(4):
        rows = slice(part * (MQ // 4), (part + 1) * (MQ // 4))
        out[rows, :] = multiply(a_full, b, rows).astype(BF)
    if q == 0:
        out[MQ : MQ + TAIL, :] = jnp.zeros((TAIL, 512), BF)
        out[MQ : MQ + TAIL, 0:128] = mask_rows(tails).astype(BF)


def scratches():
    return [VMEM((MQ, 1024), BF), VMEM((8, TAIL, 128), BF), pltpu.SemaphoreType.DMA((17,))]


def send_half(q, pieces, b):
    return pl.pallas_call(
        lambda *refs: send_kernel(q, *refs),
        out_shape=jax.ShapeDtypeStruct((rows_of(q), 512), BF),
        in_specs=[ANYWHERE] * 8 + [WHOLE],
        out_specs=WHOLE,
        scratch_shapes=scratches(),
        compiler_params=params(),
        cost_estimate=cost(2 * MQ * 1024 * 512, MQ * 1024 * 2 + 1024 * 1024),
    )(*pieces, b)


def keep_kernel(q, *refs):
    pieces, b, received = refs[:8], refs[8], refs[9]
    own, behind, ahead, upper, lower = refs[10:15]
    rest = refs[15:]
    if q == 0:
        mask, rest = rest[0], rest[1:]
    a_full, tails, sems, other = rest
    load(q, pieces, a_full, sems, tails, [(received, other)])
    for part in range(4):
        rows = slice(part * (MQ // 4), (part + 1) * (MQ // 4))
        value = multiply(a_full, b, rows) + other[rows, :].astype(F32)
        own[rows, :] = value[:, 0:128]
        ahead[rows, :] = value[:, 128:256]
        behind[rows, :] = value[:, 384:512]
        half = upper if part < 2 else lower
        at = (part % 2) * (MQ // 4)
        half[at : at + MQ // 4, :] = value[:, 256:384].astype(BF)
    if q == 0:
        mask[...] = mask_rows(tails) + other[MQ : MQ + TAIL, 0:128].astype(F32)


def keep_half(q, pieces, b, received):
    shapes = [jax.ShapeDtypeStruct((MQ, 128), F32)] * 3 + [jax.ShapeDtypeStruct((MQ // 2, 128), BF)] * 2
    if q == 0:
        shapes.append(jax.ShapeDtypeStruct((TAIL, 128), F32))
    return pl.pallas_call(
        lambda *refs: keep_kernel(q, *refs),
        out_shape=shapes,
        in_specs=[ANYWHERE] * 8 + [WHOLE, ANYWHERE],
        out_specs=[WHOLE] * len(shapes),
        scratch_shapes=scratches() + [VMEM((rows_of(q), 512), BF)],
        compiler_params=params(),
        cost_estimate=cost(2 * MQ * 1024 * 512, MQ * 1024 * 2 + 2 * 1024 * 1024),
    )(*pieces, b, received)


def relay_kernel(behind, ahead, upper, lower, behind_out, ahead_out):
    half = MQ // 2
    ahead_out[0:half, :] = (ahead[0:half, :] + upper[...].astype(F32)).astype(BF)
    ahead_out[half:MQ, :] = ahead[half:MQ, :].astype(BF)
    behind_out[0:half, :] = behind[0:half, :].astype(BF)
    behind_out[half:MQ, :] = (behind[half:MQ, :] + lower[...].astype(F32)).astype(BF)


def relay(behind, ahead, upper, lower):
    return pl.pallas_call(
        relay_kernel,
        out_shape=[jax.ShapeDtypeStruct((MQ, 128), BF)] * 2,
        in_specs=[WHOLE] * 4,
        out_specs=[WHOLE] * 2,
        compiler_params=params(),
        cost_estimate=cost(MQ * 128 * 2, MQ * 128 * 14),
    )(behind, ahead, upper, lower)


def sum_kernel(*refs):
    mask, parts, out, flips, turned = refs[0], refs[1:-6], refs[-6], refs[-5:-1], refs[-1]
    y = position()[0]
    size = MQ // 4
    for xb in range(4):
        for q in range(NQ):
            own, first, second = parts[3 * q : 3 * q + 3]
            for j in range(4 // NQ):
                at = xb * size + j * 128
                rows = slice(at, at + 128)
                value = own[rows, :] + first[rows, :].astype(F32) + second[rows, :].astype(F32)
                block = q * (4 // NQ) + j
                value = value * mask[xb * 4 + block : xb * 4 + block + 1, :]
                out[4 * block : 4 * block + 4, xb] = value.astype(BF).reshape(4, 32, 128)
                lanes = slice((xb * 4 + block) * 128, (xb * 4 + block + 1) * 128)
                turned[:, :, lanes] = value.T.astype(BF).reshape(4, 32, 128)
    for s in range(4):
        flips[s][...] = turned[lax.rem(y + s, 4)]


def sum_parts(mask, parts):
    return pl.pallas_call(
        sum_kernel,
        out_shape=[jax.ShapeDtypeStruct((16, 4, 32, 128), BF)] + [jax.ShapeDtypeStruct((32, 2048), BF)] * 4,
        in_specs=[WHOLE] * (1 + len(parts)),
        out_specs=[WHOLE] * 5,
        scratch_shapes=[VMEM((4, 32, 2048), BF)],
        compiler_params=params(),
        cost_estimate=cost(512 * 512 * 5, 512 * 512 * 14),
    )(mask, *parts)


def final_kernel(own, *refs):
    mirrored, out, ordered = refs[:4], refs[4], refs[5]
    y = position()[0]
    for s in range(4):
        ordered[lax.rem(y - s + 4, 4)] = mirrored[s][...]
    group = lax.broadcasted_iota(jnp.int32, (32, 128), 1) // 32
    for k_high in range(4):
        for layer in range(4):
            sources = [own[(4 * k_high + k) * 4 + layer].astype(F32) for k in range(4)]
            at = layer * 512 + k_high * 128
            for row in range(4):
                value = None
                for k in range(4):
                    shift = ((k - row) % 4) * 32
                    turned = pltpu.roll(sources[k], shift, 1) if shift else sources[k]
                    value = turned if value is None else jnp.where(group == k, turned, value)
                value = value + ordered[row, :, at : at + 128].astype(F32)
                out[:, row * 2048 + at : row * 2048 + at + 128] = value.astype(BF)


def finish(own, mirrored):
    return pl.pallas_call(
        final_kernel,
        out_shape=jax.ShapeDtypeStruct((32, 8192), BF),
        in_specs=[WHOLE] * 5,
        out_specs=WHOLE,
        scratch_shapes=[VMEM((4, 32, 2048), BF)],
        compiler_params=params(),
        cost_estimate=cost(32 * 8192 * 8, 3 * 32 * 8192 * 2),
    )(own, *mirrored)


def turn_z(value, shift):
    pairs = [(2 * z + c, 2 * ((z + shift) % 8) + c) for z in range(8) for c in range(2)]
    return lax.ppermute(value, "col", pairs)


def turn(value, axis, shift):
    return lax.ppermute(value, axis, [(i, (i + shift) % 4) for i in range(4)])


def per_device(density, response, density_mask, response_mask, result_mask):
    chunks = prep_a(density.reshape(2048, 128), density_mask.reshape(1, 16), result_mask.T)
    chunks, response = lax.optimization_barrier((chunks, response))
    b_send = prep_b(response.reshape(512, 512), response_mask.reshape(4, 4))

    b_own = lax.all_to_all(b_send, "col", 0, 0)
    gathered = [{0: chunk} for chunk in chunks]

    def ring(q, step):
        got = gathered[q]
        if step < 4 or q % 2 == 0:
            got[step] = turn_z(got[step - 1], 1)
        if step < 4 or q % 2 == 1:
            got[8 - step] = turn_z(got[(9 - step) % 8], -1)

    ring(0, 1)
    ring(1, 1)
    behind, ahead = turn(b_own, "row", 1), turn(b_own, "row", -1)
    ring(0, 2)
    ring(1, 2)
    (gathered[1][2], gathered[1][6], behind, ahead) = lax.optimization_barrier((gathered[1][2], gathered[1][6], behind, ahead))
    bs = [b_own, behind, ahead, turn(behind[:8], "row", 1), turn(ahead[8:], "row", -1)]
    ring(0, 3)
    ring(1, 3)
    ring(0, 4)
    ring(1, 4)

    bs = [value.reshape(-1, 4, 2, 32, 256) for value in bs]

    kept_b, sent_b = arrange(bs)

    parts = []
    mask = None
    for q in range(NQ):
        pieces = [gathered[q][s] for s in range(8)]
        other = send_half(q, pieces, sent_b)
        received = lax.ppermute(other, "col", [(i, i ^ 1) for i in range(16)])
        kept = keep_half(q, pieces, kept_b, received)
        if q == 0:
            mask = kept[5]
        own_part, back, front, upper, lower = kept[:5]
        back, front = relay(back, front, turn(upper, "layer", 1), turn(lower, "layer", -1))
        parts += [own_part, turn(front, "layer", 1), turn(back, "layer", -1)]

    product, *flips = sum_parts(mask, parts)
    own = lax.all_to_all(product.reshape(64, 32, 128), ("col", "layer"), 0, 0)
    mirrored = [flips[0]] + [turn(flips[s], "row", s) for s in (1, 2, 3)]
    return finish(own, mirrored).reshape(1, 1, 32, 8192)


def solution(mesh):
    placed = (
        P("row", "layer", "col"),
        P("layer", "row", "col"),
        P("row", "layer", "col"),
        P("layer", "row", "col"),
        P("row", "col"),
    )
    return jax.shard_map(
        per_device,
        mesh=mesh,
        in_specs=placed,
        out_specs=P(("row", "layer"), "col", None, None),
        check_vma=False,
    )
```
